128 devices in a mesh: cluster: 8 (over y, core), shard: 16 (over z, x).
Axes of the slice: x: 4, y: 4, z: 4, core: 2. Of those that a mesh axis runs over, the one named last changes fastest.
Arguments:
- documents: bfloat16 [65536, 1024], P(('cluster', 'shard'))
- partners: int32 [128, 4], P(('cluster', 'shard')), may hold values from 0 to 31, as said below
- counts: int32 [128], P(('cluster', 'shard')), may hold values from 64 to 512
Outputs:
- nearest: float32 [65536], P(('cluster', 'shard'))
The draws below stay inside these ranges and needn't reach their ends.
Inputs may be any that keep to these rules, and one draw needn't show every extreme that they name: partners[k, 0] = k mod 16, a block's pair with itself; every code names a block of its own group (below 16) or of the next group in cyclic order.
All inputs are finite; a program needn't handle non-finite values.
Results may differ from the reference program's by a relative error of at most 0.00063.
Values may be sent and summed in bfloat16 or wider, within the bound.
No kernel may reach another device: no remote copies, remote signals or barrier semaphores. Data moves between devices by JAX's collectives and lax.ppermute only.
A program may use at most 128 MiB of HBM per device.

```python
import math
import jax
import jax.numpy as jnp
from jax import lax

ROWS = 512
D = 1024
PAIRS = 4
GROUP = 16
BLOCKS = 128


def draw_documents(key, part):
    key = jax.random.fold_in(key, 11)
    keys = jax.random.split(key, 6)
    total = BLOCKS * ROWS
    groups = BLOCKS // GROUP
    pool = jax.random.normal(keys[0], (groups * 4 * ROWS, D), jnp.float32)
    pick = jax.random.randint(keys[1], (total,), 0, 4 * ROWS)
    hop = jax.random.randint(keys[2], (total,), 0, 2)
    grp = jnp.arange(total) // (ROWS * GROUP)
    source = (grp + hop) % groups * 4 * ROWS + pick
    mix = jnp.exp(jax.random.uniform(keys[3], (total, 1), jnp.float32, math.log(0.3), math.log(3.0)))
    noise = jax.random.normal(keys[4], (total, D), jnp.float32)
    scale = jnp.exp(jax.random.uniform(keys[5], (total, 1), jnp.float32, math.log(0.5), math.log(2.0)))
    return ((mix * pool[source] + noise) * scale).astype(jnp.bfloat16)


def draw_partners(key, part):
    key = jax.random.fold_in(key, 7)
    keys = jax.random.split(key, 2)
    first = jax.random.randint(keys[0], (BLOCKS, PAIRS - 1), 0, 2 * GROUP)
    second = jax.random.randint(keys[1], (BLOCKS, PAIRS - 1), 0, 2 * GROUP)
    itself = (jnp.arange(BLOCKS, dtype=jnp.int32) % GROUP)[:, None]
    return jnp.concatenate([itself, jnp.minimum(first, second).astype(jnp.int32)], axis=1)


def with_ends(result, stream_key, low, top_value):
    dims = result.shape
    index_at = [jax.random.randint(jax.random.fold_in(stream_key, axis), (), 0, dims[axis]) for axis in range(len(dims))]
    result = result.at[tuple(index_at)].set(low)
    longest = dims.index(max(dims))
    index_at[longest] = (index_at[longest] + 1) % dims[longest]
    return result.at[tuple(index_at)].set(top_value)


def setup_inputs(seed: int = 0) -> dict:
    key_of = jax.random.split(jax.random.key(seed), 4)
    return {
        "documents": draw_documents(jax.random.fold_in(key_of[3], 71), 0),
        "partners": draw_partners(jax.random.fold_in(key_of[3], 71), 0),
        "counts": with_ends(jax.random.randint(key_of[2], (BLOCKS,), ROWS // 8, ROWS + 1), jax.random.fold_in(key_of[2], 1), ROWS // 8, ROWS).astype(jnp.int32),
    }


def reference(documents, partners, counts):
    groups = BLOCKS // GROUP
    raw = documents.astype(jnp.float32)
    inv = lax.rsqrt(lax.optimization_barrier(jnp.sum(raw * raw, axis=1, keepdims=True)) + 1e-06)
    unit = (raw * inv).astype(jnp.bfloat16).reshape(BLOCKS, ROWS, D)
    owner = jnp.arange(BLOCKS, dtype=jnp.int32)[:, None] * jnp.ones((1, PAIRS), jnp.int32)
    grp = owner // GROUP
    target = jnp.where(partners < GROUP, grp * GROUP + partners, (grp + 1) % groups * GROUP + partners - GROUP).astype(jnp.int32)
    firsts = owner.reshape(-1)
    seconds = target.reshape(-1)
    slots = jnp.arange(ROWS, dtype=jnp.int32)

    def visit(best, pair):
        left, right = (pair[0], pair[1])
        scores = jnp.dot(unit[left], unit[right].T, preferred_element_type=jnp.float32)
        same = jnp.logical_and(left == right, slots[:, None] == slots[None, :])
        row_ok = slots < counts[left]
        col_ok = slots < counts[right]
        row_best = lax.optimization_barrier(jnp.max(jnp.where(jnp.logical_and(col_ok[None, :], jnp.logical_not(same)), scores, -1.0), axis=1))
        col_best = lax.optimization_barrier(jnp.max(jnp.where(jnp.logical_and(row_ok[:, None], jnp.logical_not(same)), scores, -1.0), axis=0))
        best = best.at[left].max(row_best)
        best = best.at[right].max(col_best)
        return (best, 0)
    start = jnp.full((BLOCKS, ROWS), -1.0, jnp.float32)
    best, unused = lax.scan(visit, start, jnp.stack([firsts, seconds], axis=1))
    valid = slots[None, :] < counts[:, None]
    return jnp.where(valid, best, 0.0).reshape(-1)
```

```python
import functools

import jax
import jax.numpy as jnp
from jax import lax
from jax.experimental import pallas as pl
from jax.experimental.pallas import tpu as pltpu
from jax.sharding import PartitionSpec as P

ROWS = 512
D = 1024
PAIRS = 4
SLOTS = PAIRS - 1
GROUP = 16
CUT = ROWS // GROUP
WIDE = D + 128
VMEM = pl.BlockSpec(memory_space=pltpu.VMEM)
SMEM = pl.BlockSpec(memory_space=pltpu.SMEM)


def normalise(doc_ref, row_ref, out_ref):
    raw = doc_ref[...].astype(jnp.float32)
    inv = lax.rsqrt(jnp.sum(raw * raw, axis=1, keepdims=True) + 1e-06)
    out_ref[:, :D] = (raw * inv).astype(jnp.bfloat16)
    out_ref[:, D:] = jnp.broadcast_to(row_ref[...], (doc_ref.shape[0], WIDE - D)).astype(jnp.bfloat16)


def pick(code_ref, own_ref, next_ref, out_ref):
    def one(e, carry):
        code = code_ref[e]
        dst, slot = e // SLOTS, e % SLOTS

        @pl.when(code < GROUP)
        def _():
            out_ref[dst, slot] = own_ref[code, :, :D]

        @pl.when(code >= GROUP)
        def _():
            out_ref[dst, slot] = next_ref[code - GROUP, :, :D]

        return carry

    lax.fori_loop(0, GROUP * SLOTS, one, 0)


def pair_scores(info_ref, unit_ref, got_ref, best_ref, send_ref):
    mine, count = info_ref[0], info_ref[1]
    unit = unit_ref[:, :D]
    row = lax.broadcasted_iota(jnp.int32, (ROWS, 1), 0)
    col = lax.broadcasted_iota(jnp.int32, (1, ROWS), 1)
    row_ok = row < count
    send_ref[...] = jnp.full(send_ref.shape, -1.0, jnp.float32)
    part = jnp.full((ROWS, 128), -1.0, jnp.float32)
    for p in range(SLOTS + 1):
        if p == 0:
            other, code, other_count = unit, mine, count
        else:
            other = got_ref[:, p - 1].reshape(ROWS, D)
            code, other_count = info_ref[1 + p], info_ref[4 + p]
        scores = lax.dot_general(unit, other, (((1,), (1,)), ((), ())), preferred_element_type=jnp.float32)
        off = jnp.where(code == mine, 0, ROWS)
        scores = jnp.where(row + off == col, -1.0, scores)
        rows = jnp.where(col < other_count, scores, -1.0)
        for t in range(ROWS // 128):
            part = jnp.maximum(part, rows[:, t * 128 : (t + 1) * 128])
        if p > 0:
            cols = jnp.max(jnp.where(row_ok, scores, -1.0), axis=0, keepdims=True)
            dst, step = code % GROUP, code // GROUP
            held = send_ref[dst, pl.ds(step, 1), :]
            send_ref[dst, pl.ds(step, 1), :] = jnp.maximum(held, cols)
    best_ref[...] = jnp.max(part.T, axis=0, keepdims=True)


def shards(documents, partners, counts):
    n_cluster = lax.axis_size("cluster")
    my_shard = lax.axis_index("shard")
    down = [((j + 1) % n_cluster, j) for j in range(n_cluster)]
    up = [(j, (j + 1) % n_cluster) for j in range(n_cluster)]
    table = jnp.concatenate([partners[0], counts // 32, counts % 32]).astype(jnp.float32)
    table = jnp.pad(table, (0, WIDE - D - table.shape[0]))[None]
    step = 128
    unit = pl.pallas_call(
        normalise,
        grid=(ROWS // step,),
        in_specs=[pl.BlockSpec((step, D), lambda i: (i, 0)), pl.BlockSpec((1, WIDE - D), lambda i: (0, 0))],
        out_specs=pl.BlockSpec((step, WIDE), lambda i: (i, 0)),
        out_shape=jax.ShapeDtypeStruct((ROWS, WIDE), jnp.bfloat16),
    )(documents, table)
    own = lax.all_to_all(unit.reshape(GROUP, CUT, WIDE), "shard", 0, 0, tiled=True)
    nxt = lax.ppermute(own, "cluster", down)
    own_table = own[:, 0, D : D + 8].astype(jnp.int32)
    next_table = nxt[:, 0, D : D + 8].astype(jnp.int32)
    codes = own_table[:, 1:PAIRS].reshape(-1)
    picked = pl.pallas_call(
        pick,
        in_specs=[SMEM, VMEM, VMEM],
        out_specs=VMEM,
        out_shape=jax.ShapeDtypeStruct((GROUP, SLOTS, CUT, D), jnp.bfloat16),
        compiler_params=pltpu.CompilerParams(vmem_limit_bytes=32 * 2**20),
    )(codes, own, nxt)
    got = lax.all_to_all(picked, "shard", 0, 0, tiled=True)
    all_counts = jnp.concatenate([own_table, next_table])
    all_counts = all_counts[:, PAIRS] * 32 + all_counts[:, PAIRS + 1]
    mine = partners[0, 1:]
    info = jnp.concatenate([my_shard[None], counts, mine, all_counts[mine]]).astype(jnp.int32)
    best, send = pl.pallas_call(
        pair_scores,
        in_specs=[SMEM, VMEM, VMEM],
        out_specs=[VMEM, VMEM],
        out_shape=[
            jax.ShapeDtypeStruct((1, ROWS), jnp.float32),
            jax.ShapeDtypeStruct((GROUP, 2, ROWS), jnp.float32),
        ],
        compiler_params=pltpu.CompilerParams(vmem_limit_bytes=48 * 2**20),
    )(info, unit, got)
    back = jnp.max(lax.all_to_all(send, "shard", 0, 0, tiled=True), axis=0)
    before = lax.ppermute(back[1], "cluster", up)
    best = jnp.maximum(jnp.maximum(best[0], back[0]), before)
    return jnp.where(jnp.arange(ROWS, dtype=jnp.int32) < counts[0], best, 0.0)


def solution(mesh):
    return jax.shard_map(
        shards,
        mesh=mesh,
        in_specs=(
            P(("cluster", "shard"), None),
            P(("cluster", "shard"), None),
            P(("cluster", "shard")),
        ),
        out_specs=P(("cluster", "shard")),
        check_vma=False,
    )
```

```python
import jax
import jax.numpy as jnp
from jax import lax
from jax.experimental import pallas as pl
from jax.experimental.pallas import tpu as pltpu
from jax.sharding import PartitionSpec as P

ROWS = 512
D = 1024
PAIRS = 4
SLOTS = PAIRS - 1
GROUP = 16
CUT = ROWS // GROUP
WIDE = D + 128
ENTRY = 8
STEP = 256
VMEM = pl.BlockSpec(memory_space=pltpu.VMEM)
SMEM = pl.BlockSpec(memory_space=pltpu.SMEM)


def normalise(partners_ref, counts_ref, doc_ref, out_ref):
    raw = doc_ref[...].astype(jnp.float32)
    inv = lax.rsqrt(jnp.sum(raw * raw, axis=1, keepdims=True) + 1e-06)
    out_ref[:, :D] = (raw * inv).astype(jnp.bfloat16)
    lane = lax.broadcasted_iota(jnp.int32, (STEP, WIDE - D), 1)
    entry = jnp.where(lane == 0, partners_ref[0, 0], 0)
    for p in range(1, PAIRS):
        entry = jnp.where(lane == p, partners_ref[0, p], entry)
    entry = jnp.where(lane == PAIRS, counts_ref[0] // 32, entry)
    entry = jnp.where(lane == PAIRS + 1, counts_ref[0] % 32, entry)
    out_ref[:, D:] = entry.astype(jnp.float32).astype(jnp.bfloat16)


def pick(table_ref, odd_ref, own_ref, near_ref, far_ref, out_ref):
    def one(e, carry):
        dst, slot = e // SLOTS, e % SLOTS
        code = table_ref[dst * ENTRY + 1 + slot]

        @pl.when(code < GROUP)
        def _():
            out_ref[dst, slot] = own_ref[code, :, :D]

        @pl.when(jnp.logical_and(code >= GROUP, odd_ref[0] == 0))
        def _():
            out_ref[dst, slot] = near_ref[code - GROUP, :, :D]

        @pl.when(jnp.logical_and(code >= GROUP, odd_ref[0] == 1))
        def _():
            out_ref[dst, slot] = far_ref[code - GROUP, :, :D]

        return carry

    lax.fori_loop(0, GROUP * SLOTS, one, 0)


def products(left, right):
    return lax.dot_general(left, right, (((1,), (1,)), ((), ())), preferred_element_type=jnp.float32)


def numbers():
    row = lax.broadcasted_iota(jnp.int32, (ROWS, 1), 0)
    col = lax.broadcasted_iota(jnp.int32, (1, ROWS), 1)
    return row, col


def folded(part, rows):
    for t in range(ROWS // 128):
        part = jnp.maximum(part, rows[:, t * 128 : (t + 1) * 128])
    return part


def self_scores(counts_ref, unit_ref, best_ref):
    unit = unit_ref[:, :D]
    row, col = numbers()
    keep = jnp.logical_and(col < counts_ref[0], row != col)
    rows = jnp.where(keep, products(unit, unit), -1.0)
    best_ref[...] = jnp.max(folded(jnp.full((ROWS, 128), -1.0, jnp.float32), rows).T, axis=0, keepdims=True)


def pair_scores(place_ref, partners_ref, counts_ref, own_table_ref, next_table_ref, unit_ref, got_ref, best_ref, send_ref, over_ref):
    odd, mine = place_ref[0], place_ref[1]
    unit = unit_ref[:, :D]
    row, col = numbers()
    row_ok = row < counts_ref[0]
    send_ref[...] = jnp.full(send_ref.shape, -1.0, jnp.float32)
    over_ref[...] = jnp.full(over_ref.shape, -1.0, jnp.float32)
    part = jnp.full((ROWS, 128), -1.0, jnp.float32)
    for p in range(SLOTS):
        code = partners_ref[0, 1 + p]
        at = (code % GROUP) * ENTRY + PAIRS
        own_count = own_table_ref[at] * 32 + own_table_ref[at + 1]
        next_count = next_table_ref[at] * 32 + next_table_ref[at + 1]
        other_count = jnp.where(code < GROUP, own_count, next_count)
        scores = products(unit, got_ref[:, p].reshape(ROWS, D))
        off = jnp.where(code == mine, 0, ROWS)
        scores = jnp.where(row + off == col, -1.0, scores)
        part = folded(part, jnp.where(col < other_count, scores, -1.0))
        cols = jnp.max(jnp.where(row_ok, scores, -1.0), axis=0, keepdims=True)
        line = code + jnp.where(odd == 1, 0, GROUP)

        @pl.when(line < 2 * GROUP)
        def _():
            send_ref[line] = jnp.maximum(send_ref[line], cols)

        @pl.when(line >= 2 * GROUP)
        def _():
            over_ref[line - 2 * GROUP] = jnp.maximum(over_ref[line - 2 * GROUP], cols)

    best_ref[...] = jnp.max(part.T, axis=0, keepdims=True)


def table_of(slices):
    return slices[:, 0, D : D + ENTRY].astype(jnp.int32).reshape(-1)


def shards(documents, partners, counts):
    n_cluster = lax.axis_size("cluster")
    my_cluster, my_shard = lax.axis_index("cluster"), lax.axis_index("shard")
    odd = my_cluster % 2
    unit = pl.pallas_call(
        normalise,
        grid=(ROWS // STEP,),
        in_specs=[SMEM, SMEM, pl.BlockSpec((STEP, D), lambda i: (i, 0))],
        out_specs=pl.BlockSpec((STEP, WIDE), lambda i: (i, 0)),
        out_shape=jax.ShapeDtypeStruct((ROWS, WIDE), jnp.bfloat16),
    )(partners, counts, documents)
    own = lax.all_to_all(unit.reshape(GROUP, CUT, WIDE), "shard", 0, 0, tiled=True)
    near = lax.ppermute(own, "cluster", [(c, c ^ 1) for c in range(n_cluster)])
    far = lax.ppermute(near, "cluster", [((c + 2) % n_cluster, c) for c in range(1, n_cluster, 2)])
    self_best = pl.pallas_call(
        self_scores,
        in_specs=[SMEM, VMEM],
        out_specs=VMEM,
        out_shape=jax.ShapeDtypeStruct((1, ROWS), jnp.float32),
        cost_estimate=pl.CostEstimate(flops=2 * ROWS * ROWS * D, bytes_accessed=ROWS * WIDE * 2, transcendentals=0),
    )(counts, unit)
    own_table = table_of(own)
    next_table = jnp.where(odd == 1, table_of(far), table_of(near))
    picked = pl.pallas_call(
        pick,
        in_specs=[SMEM, SMEM, VMEM, VMEM, VMEM],
        out_specs=VMEM,
        out_shape=jax.ShapeDtypeStruct((GROUP, SLOTS, CUT, D), jnp.bfloat16),
        compiler_params=pltpu.CompilerParams(vmem_limit_bytes=16 * 2**20),
    )(own_table, odd[None], own, near, far)
    got = lax.all_to_all(picked, "shard", 0, 0, tiled=True)
    best, send, over = pl.pallas_call(
        pair_scores,
        in_specs=[SMEM] * 5 + [VMEM] * 2,
        out_specs=[VMEM] * 3,
        out_shape=[
            jax.ShapeDtypeStruct((1, ROWS), jnp.float32),
            jax.ShapeDtypeStruct((2 * GROUP, 1, ROWS), jnp.float32),
            jax.ShapeDtypeStruct((GROUP, 1, ROWS), jnp.float32),
        ],
        compiler_params=pltpu.CompilerParams(vmem_limit_bytes=12 * 2**20),
    )(jnp.stack([odd, my_shard]), partners, counts, own_table, next_table, unit, got)
    over = lax.ppermute(over, "cluster", [(c, c + 1) for c in range(0, n_cluster, 2)])
    first = jnp.where(odd == 1, jnp.maximum(send[:GROUP], over), send[:GROUP])
    send = jnp.concatenate([first, send[GROUP:]])
    reach = [
        [c * GROUP + s for c in (odd_one, (odd_one + 1) % n_cluster) for s in range(GROUP)]
        for odd_one in range(1, n_cluster, 2)
    ]
    back = lax.all_to_all(send, ("cluster", "shard"), 0, 0, axis_index_groups=reach, tiled=True)
    best = jnp.maximum(jnp.maximum(best[0], self_best[0]), jnp.max(back, axis=(0, 1)))
    return jnp.where(jnp.arange(ROWS, dtype=jnp.int32) < counts[0], best, 0.0)


def solution(mesh):
    return jax.shard_map(
        shards,
        mesh=mesh,
        in_specs=(
            P(("cluster", "shard"), None),
            P(("cluster", "shard"), None),
            P(("cluster", "shard")),
        ),
        out_specs=P(("cluster", "shard")),
        check_vma=False,
    )
```

```python
import jax
import jax.numpy as jnp
from jax import lax
from jax.experimental import pallas as pl
from jax.experimental.pallas import tpu as pltpu
from jax.sharding import PartitionSpec as P

ROWS = 512
D = 1024
PAIRS = 4
SLOTS = PAIRS - 1
GROUP = 16
CUT = ROWS // GROUP
WIDE = D + 128
ENTRY = 8
HEAD = 8
STEP = 256
VMEM = pl.BlockSpec(memory_space=pltpu.VMEM)
SMEM = pl.BlockSpec(memory_space=pltpu.SMEM)


def normalise(partners_ref, counts_ref, doc_ref, out_ref):
    raw = doc_ref[...].astype(jnp.float32)
    inv = lax.rsqrt(jnp.sum(raw * raw, axis=1, keepdims=True) + 1e-06)
    out_ref[:, :D] = (raw * inv).astype(jnp.bfloat16)
    lane = lax.broadcasted_iota(jnp.int32, (STEP, WIDE - D), 1)
    entry = jnp.where(lane == 0, partners_ref[0, 0], 0)
    for p in range(1, PAIRS):
        entry = jnp.where(lane == p, partners_ref[0, p], entry)
    entry = jnp.where(lane == PAIRS, counts_ref[0] // 32, entry)
    entry = jnp.where(lane == PAIRS + 1, counts_ref[0] % 32, entry)
    out_ref[:, D:] = entry.astype(jnp.float32).astype(jnp.bfloat16)


def pick(table_ref, odd_ref, own_ref, near_ref, far_ref, out_ref):
    def one(e, carry):
        dst, slot = e // SLOTS, e % SLOTS
        code = table_ref[dst * ENTRY + 1 + slot]

        @pl.when(code < GROUP)
        def _():
            out_ref[dst, slot] = own_ref[code, :, :D]

        @pl.when(jnp.logical_and(code >= GROUP, odd_ref[0] == 0))
        def _():
            out_ref[dst, slot] = near_ref[code - GROUP, :, :D]

        @pl.when(jnp.logical_and(code >= GROUP, odd_ref[0] == 1))
        def _():
            out_ref[dst, slot] = far_ref[code - GROUP, :, :D]

        return carry

    lax.fori_loop(0, GROUP * SLOTS, one, 0)


def products(left, right):
    return lax.dot_general(left, right, (((1,), (1,)), ((), ())), preferred_element_type=jnp.float32)


def numbers():
    row = lax.broadcasted_iota(jnp.int32, (ROWS, 1), 0)
    col = lax.broadcasted_iota(jnp.int32, (1, ROWS), 1)
    return row, col


def folded(part, rows):
    for t in range(ROWS // 128):
        part = jnp.maximum(part, rows[:, t * 128 : (t + 1) * 128])
    return part


def self_scores(counts_ref, unit_ref, best_ref):
    unit = unit_ref[:, :D]
    row, col = numbers()
    keep = jnp.logical_and(col < counts_ref[0], row != col)
    rows = jnp.where(keep, products(unit, unit), -1.0)
    best_ref[...] = jnp.max(folded(jnp.full((ROWS, 128), -1.0, jnp.float32), rows).T, axis=0, keepdims=True)


def pair_scores(info_ref, unit_ref, got_ref, best_ref, send_ref, over_ref):
    odd, mine = info_ref[0], info_ref[1]
    unit = unit_ref[:, :D]
    row, col = numbers()
    row_ok = row < info_ref[2 + PAIRS]
    send_ref[...] = jnp.full(send_ref.shape, -1.0, jnp.float32)
    over_ref[...] = jnp.full(over_ref.shape, -1.0, jnp.float32)
    part = jnp.full((ROWS, 128), -1.0, jnp.float32)
    for p in range(SLOTS):
        code = info_ref[3 + p]
        at = HEAD + code * ENTRY + PAIRS
        other_count = info_ref[at] * 32 + info_ref[at + 1]
        scores = products(unit, got_ref[:, p].reshape(ROWS, D))
        off = jnp.where(code == mine, 0, ROWS)
        scores = jnp.where(row + off == col, -1.0, scores)
        part = folded(part, jnp.where(col < other_count, scores, -1.0))
        cols = jnp.max(jnp.where(row_ok, scores, -1.0), axis=0, keepdims=True)
        line = code + jnp.where(odd == 1, 0, GROUP)

        @pl.when(line < 2 * GROUP)
        def _():
            send_ref[line] = jnp.maximum(send_ref[line], cols)

        @pl.when(line >= 2 * GROUP)
        def _():
            over_ref[line - 2 * GROUP] = jnp.maximum(over_ref[line - 2 * GROUP], cols)

    best_ref[...] = jnp.max(part.T, axis=0, keepdims=True)


def table_of(slices):
    return slices[:, 0, D : D + ENTRY].astype(jnp.int32).reshape(-1)


def shards(documents, partners, counts):
    n_cluster = lax.axis_size("cluster")
    my_cluster, my_shard = lax.axis_index("cluster"), lax.axis_index("shard")
    odd = my_cluster % 2
    unit = pl.pallas_call(
        normalise,
        grid=(ROWS // STEP,),
        in_specs=[SMEM, SMEM, pl.BlockSpec((STEP, D), lambda i: (i, 0))],
        out_specs=pl.BlockSpec((STEP, WIDE), lambda i: (i, 0)),
        out_shape=jax.ShapeDtypeStruct((ROWS, WIDE), jnp.bfloat16),
    )(partners, counts, documents)
    own = lax.all_to_all(unit.reshape(GROUP, CUT, WIDE), "shard", 0, 0, tiled=True)
    near = lax.ppermute(own, "cluster", [(c, c ^ 1) for c in range(n_cluster)])
    far = lax.ppermute(near, "cluster", [((c + 2) % n_cluster, c) for c in range(1, n_cluster, 2)])
    own_table = table_of(own)
    next_table = jnp.where(odd == 1, table_of(far), table_of(near))
    picked = pl.pallas_call(
        pick,
        in_specs=[SMEM, SMEM, VMEM, VMEM, VMEM],
        out_specs=VMEM,
        out_shape=jax.ShapeDtypeStruct((GROUP, SLOTS, CUT, D), jnp.bfloat16),
        compiler_params=pltpu.CompilerParams(vmem_limit_bytes=16 * 2**20),
    )(own_table, odd[None], own, near, far)
    head = jnp.concatenate([odd[None], my_shard[None], partners[0], counts, jnp.zeros((1,), jnp.int32)])
    picked, info = lax.optimization_barrier((picked, jnp.concatenate([head, own_table, next_table])))
    got = lax.all_to_all(picked, "shard", 0, 0, tiled=True)
    best, send, over = pl.pallas_call(
        pair_scores,
        in_specs=[SMEM, VMEM, VMEM],
        out_specs=[VMEM] * 3,
        out_shape=[
            jax.ShapeDtypeStruct((1, ROWS), jnp.float32),
            jax.ShapeDtypeStruct((2 * GROUP, 1, ROWS), jnp.float32),
            jax.ShapeDtypeStruct((GROUP, 1, ROWS), jnp.float32),
        ],
        compiler_params=pltpu.CompilerParams(vmem_limit_bytes=12 * 2**20),
    )(info, unit, got)
    later, count, send, over, best = lax.optimization_barrier((unit, counts, send, over, best))
    self_best = pl.pallas_call(
        self_scores,
        in_specs=[SMEM, VMEM],
        out_specs=VMEM,
        out_shape=jax.ShapeDtypeStruct((1, ROWS), jnp.float32),
        cost_estimate=pl.CostEstimate(flops=2 * ROWS * ROWS * D, bytes_accessed=ROWS * WIDE * 2, transcendentals=0),
    )(count, later)
    over = lax.ppermute(over, "cluster", [(c, c + 1) for c in range(0, n_cluster, 2)])
    first = jnp.where(odd == 1, jnp.maximum(send[:GROUP], over), send[:GROUP])
    send = jnp.concatenate([first, send[GROUP:]])
    reach = [
        [c * GROUP + s for c in (odd_one, (odd_one + 1) % n_cluster) for s in range(GROUP)]
        for odd_one in range(1, n_cluster, 2)
    ]
    back = lax.all_to_all(send, ("cluster", "shard"), 0, 0, axis_index_groups=reach, tiled=True)
    best = jnp.maximum(jnp.maximum(best[0], self_best[0]), jnp.max(back, axis=(0, 1)))
    return jnp.where(jnp.arange(ROWS, dtype=jnp.int32) < counts[0], best, 0.0)


def solution(mesh):
    return jax.shard_map(
        shards,
        mesh=mesh,
        in_specs=(
            P(("cluster", "shard"), None),
            P(("cluster", "shard"), None),
            P(("cluster", "shard")),
        ),
        out_specs=P(("cluster", "shard")),
        check_vma=False,
    )
```

```python
import jax
import jax.numpy as jnp
from jax import lax
from jax.experimental import pallas as pl
from jax.experimental.pallas import tpu as pltpu
from jax.sharding import PartitionSpec as P

ROWS = 512
D = 1024
PAIRS = 4
SLOTS = PAIRS - 1
GROUP = 16
CUT = ROWS // GROUP
WIDE = D + 128
STEP = 128
VMEM = pl.BlockSpec(memory_space=pltpu.VMEM)
SMEM = pl.BlockSpec(memory_space=pltpu.SMEM)
ANY = pl.BlockSpec(memory_space=pl.ANY)


def unit_rows(raw):
    raw = raw.astype(jnp.float32)
    return raw * lax.rsqrt(jnp.sum(raw * raw, axis=1, keepdims=True) + 1e-06)


def normalise(partners_ref, counts_ref, doc_ref, out_ref, raw, unit, partners, counts, in_sem, out_sem, small_sem):
    small = [
        pltpu.make_async_copy(partners_ref, partners, small_sem.at[0]),
        pltpu.make_async_copy(counts_ref, counts, small_sem.at[1]),
    ]
    fetch = [
        pltpu.make_async_copy(doc_ref.at[pl.ds(i, STEP)], raw.at[pl.ds(i, STEP)], in_sem.at[i // STEP])
        for i in range(0, ROWS, STEP)
    ]
    store = [
        pltpu.make_async_copy(unit.at[pl.ds(i, STEP)], out_ref.at[pl.ds(i, STEP)], out_sem.at[i // STEP])
        for i in range(0, ROWS, STEP)
    ]
    for copy in small + fetch:
        copy.start()
    for copy in small:
        copy.wait()
    lane = lax.broadcasted_iota(jnp.int32, (16, WIDE - D), 1)
    entry = jnp.where(lane == 0, partners[0, 0], 0)
    for p in range(1, PAIRS):
        entry = jnp.where(lane == p, partners[0, p], entry)
    entry = entry.astype(jnp.float32).astype(jnp.bfloat16)
    for i in range(0, ROWS, STEP):
        fetch[i // STEP].wait()
        rows = unit_rows(raw[i : i + STEP])
        if i == 0:
            first = rows[:1]
        row = i + lax.broadcasted_iota(jnp.int32, (STEP, 1), 0)
        unit[i : i + STEP, :D] = jnp.where(row < counts[0], rows, first).astype(jnp.bfloat16)
        for j in range(i, i + STEP, 16):
            unit[j : j + 16, D:] = entry
        store[i // STEP].start()
    for copy in store:
        copy.wait()


def pick(table_ref, odd_ref, own_ref, near_ref, far_ref, out_ref):
    def all_from(next_ref):
        for e in range(GROUP * SLOTS):
            dst, slot = e // SLOTS, e % SLOTS
            code = table_ref[dst * PAIRS + 1 + slot]

            @pl.when(code < GROUP)
            def _():
                out_ref[dst, slot] = own_ref[code, :, :D]

            @pl.when(code >= GROUP)
            def _():
                out_ref[dst, slot] = next_ref[code - GROUP, :, :D]

    @pl.when(odd_ref[0] == 0)
    def _():
        all_from(near_ref)

    @pl.when(odd_ref[0] == 1)
    def _():
        all_from(far_ref)


def products(left, right):
    return lax.dot_general(left, right, (((1,), (1,)), ((), ())), preferred_element_type=jnp.float32)


def folded(part, rows):
    for t in range(rows.shape[1] // 128):
        part = jnp.maximum(part, rows[:, t * 128 : (t + 1) * 128])
    return part


def self_scores(counts_ref, unit_ref, best_ref):
    unit = unit_ref[:, :D]
    row = lax.broadcasted_iota(jnp.int32, (ROWS, 1), 0)
    col = lax.broadcasted_iota(jnp.int32, (1, ROWS), 1)
    keep = jnp.logical_and(col < counts_ref[0], row != col)
    rows = jnp.where(keep, products(unit, unit), -1.0)
    best_ref[...] = jnp.max(folded(jnp.full((ROWS, 128), -1.0, jnp.float32), rows).T, axis=0, keepdims=True)


def pair_scores(info_ref, unit_ref, got_ref, best_ref, send_ref, over_ref=None):
    odd, mine = info_ref[0], info_ref[1]
    unit = unit_ref[:, :D]
    send_ref[...] = jnp.full(send_ref.shape, -1.0, jnp.float32)
    part = jnp.full((ROWS, 128), -1.0, jnp.float32)
    for p in range(SLOTS):
        code = info_ref[3 + p]
        twice = code == mine
        scores = products(unit, got_ref[:, p].reshape(ROWS, D))
        part = jnp.where(twice, part, folded(part, scores))
        cols = jnp.where(twice, -1.0, jnp.max(scores, axis=0, keepdims=True))
        line = code + jnp.where(odd == 1, 0, GROUP)

        @pl.when(line < 2 * GROUP)
        def _():
            send_ref[line] = jnp.maximum(send_ref[line], cols)

        if over_ref is not None:

            @pl.when(line >= 2 * GROUP)
            def _():
                over_ref[line - 2 * GROUP] = jnp.maximum(over_ref[line - 2 * GROUP], cols)

    best_ref[...] = jnp.max(part.T, axis=0, keepdims=True)


def even_scores(info_ref, unit_ref, got_ref, best_ref, send_ref, over_ref):
    over_ref[...] = jnp.full(over_ref.shape, -1.0, jnp.float32)

    @pl.when(info_ref[0] == 0)
    def _():
        pair_scores(info_ref, unit_ref, got_ref, best_ref, send_ref, over_ref)


def odd_scores(info_ref, unit_ref, got_ref, held_best_ref, held_send_ref, best_ref, send_ref):
    @pl.when(info_ref[0] == 1)
    def _():
        pair_scores(info_ref, unit_ref, got_ref, best_ref, send_ref)

    @pl.when(info_ref[0] == 0)
    def _():
        best_ref[...] = held_best_ref[...]
        send_ref[...] = held_send_ref[...]


def shards(documents, partners, counts):
    n_cluster = lax.axis_size("cluster")
    my_cluster, my_shard = lax.axis_index("cluster"), lax.axis_index("shard")
    odd = my_cluster % 2
    unit = pl.pallas_call(
        normalise,
        in_specs=[ANY] * 3,
        out_specs=ANY,
        out_shape=jax.ShapeDtypeStruct((ROWS, WIDE), jnp.bfloat16),
        scratch_shapes=[
            pltpu.VMEM((ROWS, D), jnp.bfloat16),
            pltpu.VMEM((ROWS, WIDE), jnp.bfloat16),
            pltpu.SMEM((1, PAIRS), jnp.int32),
            pltpu.SMEM((1,), jnp.int32),
            pltpu.SemaphoreType.DMA((ROWS // STEP,)),
            pltpu.SemaphoreType.DMA((ROWS // STEP,)),
            pltpu.SemaphoreType.DMA((2,)),
        ],
    )(partners, counts, documents)
    own = lax.all_to_all(unit.reshape(GROUP, CUT, WIDE), "shard", 0, 0, tiled=True)
    near = lax.ppermute(own, "cluster", [(c, c ^ 1) for c in range(n_cluster)])
    far = lax.ppermute(near, "cluster", [((c + 2) % n_cluster, c) for c in range(1, n_cluster, 2)])
    table = own[:, 0, D : D + PAIRS].astype(jnp.int32).reshape(-1)
    picked = pl.pallas_call(
        pick,
        in_specs=[SMEM, SMEM, VMEM, VMEM, VMEM],
        out_specs=VMEM,
        out_shape=jax.ShapeDtypeStruct((GROUP, SLOTS, CUT, D), jnp.bfloat16),
        compiler_params=pltpu.CompilerParams(vmem_limit_bytes=16 * 2**20),
    )(table, odd[None], own, near, far)
    info = jnp.concatenate([odd[None], my_shard[None], partners[0]])
    picked, info, is_odd = lax.optimization_barrier((picked, info, odd == 1))
    got = lax.all_to_all(picked, "shard", 0, 0, tiled=True)
    best_shape = jax.ShapeDtypeStruct((1, ROWS), jnp.float32)
    send_shape = jax.ShapeDtypeStruct((2 * GROUP, 1, ROWS), jnp.float32)
    over_shape = jax.ShapeDtypeStruct((GROUP, 1, ROWS), jnp.float32)
    params = pltpu.CompilerParams(vmem_limit_bytes=12 * 2**20)
    best, send, over = pl.pallas_call(
        even_scores,
        in_specs=[SMEM, VMEM, VMEM],
        out_specs=[VMEM] * 3,
        out_shape=[best_shape, send_shape, over_shape],
        compiler_params=params,
    )(info, unit, got)
    over = lax.ppermute(over, "cluster", [(c, c + 1) for c in range(0, n_cluster, 2)])
    best, send = pl.pallas_call(
        odd_scores,
        in_specs=[SMEM] + [VMEM] * 4,
        out_specs=[VMEM] * 2,
        out_shape=[best_shape, send_shape],
        input_output_aliases={3: 0, 4: 1},
        compiler_params=params,
        cost_estimate=pl.CostEstimate(flops=SLOTS * 2 * ROWS * ROWS * D, bytes_accessed=4 * ROWS * D * 2, transcendentals=0),
    )(info, unit, got, best, send)
    later, count, send, best = lax.optimization_barrier((unit, counts, send, best))
    self_best = pl.pallas_call(
        self_scores,
        in_specs=[SMEM, VMEM],
        out_specs=VMEM,
        out_shape=jax.ShapeDtypeStruct((1, ROWS), jnp.float32),
        cost_estimate=pl.CostEstimate(flops=2 * ROWS * ROWS * D, bytes_accessed=ROWS * WIDE * 2, transcendentals=0),
    )(count, later)
    first = jnp.where(is_odd, jnp.maximum(send[:GROUP], over), send[:GROUP])
    send = jnp.concatenate([first, send[GROUP:]])
    reach = [
        [c * GROUP + s for c in (odd_one, (odd_one + 1) % n_cluster) for s in range(GROUP)]
        for odd_one in range(1, n_cluster, 2)
    ]
    back = lax.all_to_all(send, ("cluster", "shard"), 0, 0, axis_index_groups=reach, tiled=True)
    best = jnp.maximum(jnp.maximum(best[0], self_best[0]), jnp.max(back, axis=(0, 1)))
    return jnp.where(jnp.arange(ROWS, dtype=jnp.int32) < counts[0], best, 0.0)


def solution(mesh):
    return jax.shard_map(
        shards,
        mesh=mesh,
        in_specs=(
            P(("cluster", "shard"), None),
            P(("cluster", "shard"), None),
            P(("cluster", "shard")),
        ),
        out_specs=P(("cluster", "shard")),
        check_vma=False,
    )
```

```python
import jax
import jax.numpy as jnp
from jax import lax
from jax.experimental import pallas as pl
from jax.experimental.pallas import tpu as pltpu
from jax.sharding import PartitionSpec as P

ROWS = 512
D = 1024
PAIRS = 4
SLOTS = PAIRS - 1
GROUP = 16
CUT = ROWS // GROUP
LANES = 128
TILES = D // LANES
BODY = TILES * CUT
TALL = BODY + 16
STEP = 128
ORDER = [10, 15, 13, 11, 2, 14, 6, 7, 0, 9, 5, 4, 8, 1, 3, 12]
REACH = ORDER
PLACE = [ORDER.index(s) for s in range(GROUP)]
REACH_PLACE = [REACH.index(s) for s in range(GROUP)]
VMEM = pl.BlockSpec(memory_space=pltpu.VMEM)
SMEM = pl.BlockSpec(memory_space=pltpu.SMEM)
ANY = pl.BlockSpec(memory_space=pl.ANY)


def moved(code, places):
    shard = code % GROUP
    place = shard
    for s in range(GROUP):
        place = jnp.where(shard == s, places[s], place)
    return place + code - shard


def by_place(code):
    return moved(code, PLACE)


def to_reach(code):
    return moved(code, REACH_PLACE)


def unit_rows(raw):
    raw = raw.astype(jnp.float32)
    return raw * lax.rsqrt(jnp.sum(raw * raw, axis=1, keepdims=True) + 1e-06)


def normalise(partners_ref, counts_ref, doc_ref, out_ref, raw, unit, partners, counts, in_sem, out_sem, small_sem):
    small = [
        pltpu.make_async_copy(partners_ref, partners, small_sem.at[0]),
        pltpu.make_async_copy(counts_ref, counts, small_sem.at[1]),
    ]
    fetch = [
        pltpu.make_async_copy(doc_ref.at[pl.ds(i, STEP)], raw.at[pl.ds(i, STEP)], in_sem.at[i // STEP])
        for i in range(0, ROWS, STEP)
    ]
    store = [
        pltpu.make_async_copy(unit.at[pl.ds(i, STEP // CUT)], out_ref.at[pl.ds(i, STEP // CUT)], out_sem.at[i * CUT // STEP])
        for i in range(0, GROUP, STEP // CUT)
    ]
    for copy in small + fetch:
        copy.start()
    for copy in small:
        copy.wait()
    lane = lax.broadcasted_iota(jnp.int32, (16, LANES), 1)
    entry = jnp.where(lane == 0, by_place(partners[0, 0]), 0)
    for p in range(1, PAIRS):
        entry = jnp.where(lane == p, by_place(partners[0, p]), entry)
    entry = entry.astype(jnp.float32).astype(jnp.bfloat16)
    for i in range(0, ROWS, STEP):
        fetch[i // STEP].wait()
        rows = unit_rows(raw[i : i + STEP])
        if i == 0:
            first = rows[:1]
        row = i + lax.broadcasted_iota(jnp.int32, (STEP, 1), 0)
        rows = jnp.where(row < counts[0], rows, first).astype(jnp.bfloat16)
        for j in range(0, STEP, CUT):
            at = (i + j) // CUT
            for t in range(TILES):
                unit[at, t * CUT : (t + 1) * CUT] = rows[j : j + CUT, t * LANES : (t + 1) * LANES]
            unit[at, BODY:] = entry
        store[i // STEP].start()
    for copy in store:
        copy.wait()


def pick(table_ref, odd_ref, own_ref, near_ref, far_ref, out_ref):
    def all_from(next_ref):
        for e in range(GROUP * SLOTS):
            dst, slot = e // SLOTS, e % SLOTS
            code = table_ref[dst * PAIRS + 1 + slot]

            @pl.when(code < GROUP)
            def _():
                out_ref[dst, slot] = own_ref[code, :BODY]

            @pl.when(code >= GROUP)
            def _():
                out_ref[dst, slot] = next_ref[code - GROUP, :BODY]

    @pl.when(odd_ref[0] == 0)
    def _():
        all_from(near_ref)

    @pl.when(odd_ref[0] == 1)
    def _():
        all_from(far_ref)


def rows_of(slices):
    tiles = [slices[:, t * CUT : (t + 1) * CUT].reshape(ROWS, LANES) for t in range(TILES)]
    return jnp.concatenate(tiles, axis=1)


def products(left, right):
    return lax.dot_general(left, right, (((1,), (1,)), ((), ())), preferred_element_type=jnp.float32)


def folded(part, rows):
    for t in range(rows.shape[1] // 128):
        part = jnp.maximum(part, rows[:, t * 128 : (t + 1) * 128])
    return part


def self_part(count, unit):
    row = lax.broadcasted_iota(jnp.int32, (ROWS, 1), 0)
    col = lax.broadcasted_iota(jnp.int32, (1, ROWS), 1)
    rows = jnp.where(jnp.logical_and(col < count, row != col), products(unit, unit), -1.0)
    return folded(jnp.full((ROWS, 128), -1.0, jnp.float32), rows)


def highest(part):
    return jnp.max(part.T, axis=0, keepdims=True)


def odd_self(info_ref, unit_ref, best_ref):
    @pl.when(info_ref[0] == 1)
    def _():
        best_ref[...] = highest(self_part(info_ref[2 + PAIRS], rows_of(unit_ref)))

    @pl.when(info_ref[0] == 0)
    def _():
        best_ref[...] = jnp.full(best_ref.shape, -1.0, jnp.float32)


def pair_scores(info_ref, unit_ref, got_ref, send_ref, over_ref=None):
    odd, mine = info_ref[0], info_ref[1]
    unit = rows_of(unit_ref)
    send_ref[...] = jnp.full(send_ref.shape, -1.0, jnp.float32)
    part = jnp.full((ROWS, 128), -1.0, jnp.float32)
    for p in range(SLOTS):
        code = info_ref[3 + p]
        twice = code == mine
        scores = products(unit, rows_of(got_ref.at[:, p]))
        part = jnp.where(twice, part, folded(part, scores))
        cols = jnp.where(twice, -1.0, jnp.max(scores, axis=0, keepdims=True))
        line = to_reach(code) + jnp.where(odd == 1, 0, GROUP)

        @pl.when(line < 2 * GROUP)
        def _():
            send_ref[line] = jnp.maximum(send_ref[line], cols)

        if over_ref is not None:

            @pl.when(line >= 2 * GROUP)
            def _():
                over_ref[line - 2 * GROUP] = jnp.maximum(over_ref[line - 2 * GROUP], cols)

    return part


def even_scores(info_ref, unit_ref, got_ref, best_ref, send_ref, over_ref):
    over_ref[...] = jnp.full(over_ref.shape, -1.0, jnp.float32)

    @pl.when(info_ref[0] == 0)
    def _():
        part = pair_scores(info_ref, unit_ref, got_ref, send_ref, over_ref)
        best_ref[...] = highest(jnp.maximum(part, self_part(info_ref[2 + PAIRS], rows_of(unit_ref))))


def odd_scores(info_ref, unit_ref, got_ref, self_ref, held_best_ref, held_send_ref, best_ref, send_ref):
    @pl.when(info_ref[0] == 1)
    def _():
        part = pair_scores(info_ref, unit_ref, got_ref, send_ref)
        best_ref[...] = jnp.maximum(highest(part), self_ref[...])

    @pl.when(info_ref[0] == 0)
    def _():
        best_ref[...] = held_best_ref[...]
        send_ref[...] = held_send_ref[...]


def exchange(parts):
    return lax.all_to_all(parts, "shard", 0, 0, axis_index_groups=[ORDER], tiled=True)


def shards(documents, partners, counts):
    n_cluster = lax.axis_size("cluster")
    my_cluster, my_shard = lax.axis_index("cluster"), lax.axis_index("shard")
    odd = my_cluster % 2
    unit = pl.pallas_call(
        normalise,
        in_specs=[ANY] * 3,
        out_specs=ANY,
        out_shape=jax.ShapeDtypeStruct((GROUP, TALL, LANES), jnp.bfloat16),
        scratch_shapes=[
            pltpu.VMEM((ROWS, D), jnp.bfloat16),
            pltpu.VMEM((GROUP, TALL, LANES), jnp.bfloat16),
            pltpu.SMEM((1, PAIRS), jnp.int32),
            pltpu.SMEM((1,), jnp.int32),
            pltpu.SemaphoreType.DMA((ROWS // STEP,)),
            pltpu.SemaphoreType.DMA((ROWS // STEP,)),
            pltpu.SemaphoreType.DMA((2,)),
        ],
    )(partners, counts, documents)
    own = exchange(unit)
    near = lax.ppermute(own, "cluster", [(c, c ^ 1) for c in range(n_cluster)])
    far = lax.ppermute(near, "cluster", [((c + 2) % n_cluster, c) for c in range(1, n_cluster, 2)])
    info = jnp.concatenate([odd[None], my_shard[None], partners[0], counts])
    held, near = lax.optimization_barrier((unit, near))
    self_best = pl.pallas_call(
        odd_self,
        in_specs=[SMEM, VMEM],
        out_specs=VMEM,
        out_shape=jax.ShapeDtypeStruct((1, ROWS), jnp.float32),
        cost_estimate=pl.CostEstimate(flops=2 * ROWS * ROWS * D, bytes_accessed=ROWS * D * 2, transcendentals=0),
        compiler_params=pltpu.CompilerParams(vmem_limit_bytes=12 * 2**20),
    )(info, held)
    table = own[:, BODY, :PAIRS].astype(jnp.int32).reshape(-1)
    picked = pl.pallas_call(
        pick,
        in_specs=[SMEM, SMEM, VMEM, VMEM, VMEM],
        out_specs=VMEM,
        out_shape=jax.ShapeDtypeStruct((GROUP, SLOTS, BODY, LANES), jnp.bfloat16),
        compiler_params=pltpu.CompilerParams(vmem_limit_bytes=16 * 2**20),
    )(table, odd[None], own, near, far)
    picked, info, self_best, is_odd = lax.optimization_barrier((picked, info, self_best, odd == 1))
    got = exchange(picked)
    best_shape = jax.ShapeDtypeStruct((1, ROWS), jnp.float32)
    send_shape = jax.ShapeDtypeStruct((2 * GROUP, 1, ROWS), jnp.float32)
    over_shape = jax.ShapeDtypeStruct((GROUP, 1, ROWS), jnp.float32)
    params = pltpu.CompilerParams(vmem_limit_bytes=12 * 2**20)
    best, send, over = pl.pallas_call(
        even_scores,
        in_specs=[SMEM, VMEM, VMEM],
        out_specs=[VMEM] * 3,
        out_shape=[best_shape, send_shape, over_shape],
        compiler_params=params,
    )(info, unit, got)
    over = lax.ppermute(over, "cluster", [(c, c + 1) for c in range(0, n_cluster, 2)])
    best, send = pl.pallas_call(
        odd_scores,
        in_specs=[SMEM] + [VMEM] * 5,
        out_specs=[VMEM] * 2,
        out_shape=[best_shape, send_shape],
        input_output_aliases={4: 0, 5: 1},
        compiler_params=params,
        cost_estimate=pl.CostEstimate(flops=SLOTS * 2 * ROWS * ROWS * D, bytes_accessed=4 * ROWS * D * 2, transcendentals=0),
    )(info, unit, got, self_best, best, send)
    first = jnp.where(is_odd, jnp.maximum(send[:GROUP], over), send[:GROUP])
    send = jnp.concatenate([first, send[GROUP:]])
    reach = [
        [c * GROUP + s for c in (odd_one, (odd_one + 1) % n_cluster) for s in REACH]
        for odd_one in range(1, n_cluster, 2)
    ]
    back = lax.all_to_all(send, ("cluster", "shard"), 0, 0, axis_index_groups=reach, tiled=True)
    best = jnp.maximum(best[0], jnp.max(back, axis=(0, 1)))
    return jnp.where(jnp.arange(ROWS, dtype=jnp.int32) < counts[0], best, 0.0)


def solution(mesh):
    return jax.shard_map(
        shards,
        mesh=mesh,
        in_specs=(
            P(("cluster", "shard"), None),
            P(("cluster", "shard"), None),
            P(("cluster", "shard")),
        ),
        out_specs=P(("cluster", "shard")),
        check_vma=False,
    )
```

```python
import jax
import jax.numpy as jnp
from jax import lax
from jax.experimental import pallas as pl
from jax.experimental.pallas import tpu as pltpu
from jax.sharding import PartitionSpec as P

ROWS = 512
D = 1024
PAIRS = 4
SLOTS = PAIRS - 1
GROUP = 16
CUT = ROWS // GROUP
LANES = 128
TILES = D // LANES
BODY = TILES * CUT
TALL = BODY + 16
STEP = 256
ORDER = [10, 15, 13, 11, 2, 14, 6, 7, 0, 9, 5, 4, 8, 1, 3, 12]
REACH = ORDER
PLACE = [ORDER.index(s) for s in range(GROUP)]
REACH_PLACE = [REACH.index(s) for s in range(GROUP)]
VMEM = pl.BlockSpec(memory_space=pltpu.VMEM)
SMEM = pl.BlockSpec(memory_space=pltpu.SMEM)
ANY = pl.BlockSpec(memory_space=pl.ANY)


def moved(code, places):
    shard = code % GROUP
    place = shard
    for s in range(GROUP):
        place = jnp.where(shard == s, places[s], place)
    return place + code - shard


def by_place(code):
    return moved(code, PLACE)


def to_reach(code):
    return moved(code, REACH_PLACE)


def unit_rows(raw):
    raw = raw.astype(jnp.float32)
    return raw * lax.rsqrt(jnp.sum(raw * raw, axis=1, keepdims=True) + 1e-06)


def normalise(partners_ref, counts_ref, doc_ref, unit, raw, partners, counts, in_sem, small_sem):
    small = [
        pltpu.make_async_copy(partners_ref, partners, small_sem.at[0]),
        pltpu.make_async_copy(counts_ref, counts, small_sem.at[1]),
    ]
    fetch = [
        pltpu.make_async_copy(doc_ref.at[pl.ds(i, STEP)], raw.at[pl.ds(i, STEP)], in_sem.at[i // STEP])
        for i in range(0, ROWS, STEP)
    ]
    for copy in small + fetch:
        copy.start()
    for copy in small:
        copy.wait()
    lane = lax.broadcasted_iota(jnp.int32, (16, LANES), 1)
    entry = jnp.where(lane == 0, by_place(partners[0, 0]), 0)
    for p in range(1, PAIRS):
        entry = jnp.where(lane == p, by_place(partners[0, p]), entry)
    entry = entry.astype(jnp.float32).astype(jnp.bfloat16)
    for i in range(0, ROWS, STEP):
        fetch[i // STEP].wait()
        rows = unit_rows(raw[i : i + STEP])
        if i == 0:
            first = rows[:1]
        row = i + lax.broadcasted_iota(jnp.int32, (STEP, 1), 0)
        rows = jnp.where(row < counts[0], rows, first).astype(jnp.bfloat16)
        for j in range(0, STEP, CUT):
            at = (i + j) // CUT
            for t in range(TILES):
                unit[at, t * CUT : (t + 1) * CUT] = rows[j : j + CUT, t * LANES : (t + 1) * LANES]
            unit[at, BODY:] = entry


def pick(table_ref, odd_ref, own_ref, near_ref, far_ref, out_ref, far, sem):
    fetch = pltpu.make_async_copy(far_ref, far, sem)

    def each(body):
        for e in range(GROUP * SLOTS):
            dst, slot = e // SLOTS, e % SLOTS
            body(dst, slot, table_ref[dst * PAIRS + 1 + slot])

    def from_own(dst, slot, code):
        @pl.when(code < GROUP)
        def _():
            out_ref[dst, slot] = own_ref[code, :BODY]

    def from_next(next_ref):
        def one(dst, slot, code):
            @pl.when(code >= GROUP)
            def _():
                out_ref[dst, slot] = next_ref[code - GROUP, :BODY]

        return one

    @pl.when(odd_ref[0] == 1)
    def _():
        fetch.start()

    each(from_own)

    @pl.when(odd_ref[0] == 0)
    def _():
        each(from_next(near_ref))

    @pl.when(odd_ref[0] == 1)
    def _():
        fetch.wait()
        each(from_next(far))


def rows_of(slices):
    tiles = [slices[:, t * CUT : (t + 1) * CUT].reshape(ROWS, LANES) for t in range(TILES)]
    return jnp.concatenate(tiles, axis=1)


def products(left, right):
    return lax.dot_general(left, right, (((1,), (1,)), ((), ())), preferred_element_type=jnp.float32)


def folded(part, rows):
    for t in range(rows.shape[1] // 128):
        part = jnp.maximum(part, rows[:, t * 128 : (t + 1) * 128])
    return part


def self_part(count, unit):
    row = lax.broadcasted_iota(jnp.int32, (ROWS, 1), 0)
    col = lax.broadcasted_iota(jnp.int32, (1, ROWS), 1)
    rows = jnp.where(jnp.logical_and(col < count, row != col), products(unit, unit), -1.0)
    return folded(jnp.full((ROWS, 128), -1.0, jnp.float32), rows)


def highest(part):
    return jnp.max(part.T, axis=0, keepdims=True)


def odd_self(info_ref, unit_ref, best_ref):
    @pl.when(info_ref[0] == 1)
    def _():
        best_ref[...] = highest(self_part(info_ref[2 + PAIRS], rows_of(unit_ref)))

    @pl.when(info_ref[0] == 0)
    def _():
        best_ref[...] = jnp.full(best_ref.shape, -1.0, jnp.float32)


def pair_scores(info_ref, unit_ref, got_ref, send_ref, over_ref=None):
    odd, mine = info_ref[0], info_ref[1]
    unit = rows_of(unit_ref)
    send_ref[...] = jnp.full(send_ref.shape, -1.0, jnp.float32)
    part = jnp.full((ROWS, 128), -1.0, jnp.float32)
    for p in range(SLOTS):
        code = info_ref[3 + p]
        twice = code == mine
        scores = products(unit, rows_of(got_ref.at[:, p]))
        part = jnp.where(twice, part, folded(part, scores))
        cols = jnp.where(twice, -1.0, jnp.max(scores, axis=0, keepdims=True))
        line = to_reach(code) + jnp.where(odd == 1, 0, GROUP)

        @pl.when(line < 2 * GROUP)
        def _():
            send_ref[line] = jnp.maximum(send_ref[line], cols)

        if over_ref is not None:

            @pl.when(line >= 2 * GROUP)
            def _():
                over_ref[line - 2 * GROUP] = jnp.maximum(over_ref[line - 2 * GROUP], cols)

    return part


def even_scores(info_ref, unit_ref, got_ref, best_ref, send_ref, over_ref):
    over_ref[...] = jnp.full(over_ref.shape, -1.0, jnp.float32)

    @pl.when(info_ref[0] == 0)
    def _():
        part = pair_scores(info_ref, unit_ref, got_ref, send_ref, over_ref)
        best_ref[...] = highest(jnp.maximum(part, self_part(info_ref[2 + PAIRS], rows_of(unit_ref))))


def odd_scores(info_ref, unit_ref, got_ref, self_ref, held_best_ref, held_send_ref, best_ref, send_ref):
    @pl.when(info_ref[0] == 1)
    def _():
        part = pair_scores(info_ref, unit_ref, got_ref, send_ref)
        best_ref[...] = jnp.maximum(highest(part), self_ref[...])

    @pl.when(info_ref[0] == 0)
    def _():
        best_ref[...] = held_best_ref[...]
        send_ref[...] = held_send_ref[...]


def exchange(parts):
    return lax.all_to_all(parts, "shard", 0, 0, axis_index_groups=[ORDER], tiled=True)


def shards(documents, partners, counts):
    n_cluster = lax.axis_size("cluster")
    my_cluster, my_shard = lax.axis_index("cluster"), lax.axis_index("shard")
    odd = my_cluster % 2
    unit = pl.pallas_call(
        normalise,
        in_specs=[ANY] * 3,
        out_specs=VMEM,
        out_shape=jax.ShapeDtypeStruct((GROUP, TALL, LANES), jnp.bfloat16),
        scratch_shapes=[
            pltpu.VMEM((ROWS, D), jnp.bfloat16),
            pltpu.SMEM((1, PAIRS), jnp.int32),
            pltpu.SMEM((1,), jnp.int32),
            pltpu.SemaphoreType.DMA((ROWS // STEP,)),
            pltpu.SemaphoreType.DMA((2,)),
        ],
        compiler_params=pltpu.CompilerParams(vmem_limit_bytes=8 * 2**20),
    )(partners, counts, documents)
    own = exchange(unit)
    near = lax.ppermute(own, "cluster", [(c, c ^ 1) for c in range(n_cluster)])
    info = jnp.concatenate([odd[None], my_shard[None], partners[0], counts])
    held, own = lax.optimization_barrier((unit, own))
    self_best = pl.pallas_call(
        odd_self,
        in_specs=[SMEM, VMEM],
        out_specs=VMEM,
        out_shape=jax.ShapeDtypeStruct((1, ROWS), jnp.float32),
        cost_estimate=pl.CostEstimate(flops=2 * ROWS * ROWS * D, bytes_accessed=ROWS * D * 2, transcendentals=0),
        compiler_params=pltpu.CompilerParams(vmem_limit_bytes=12 * 2**20),
    )(info, held)
    near, self_best = lax.optimization_barrier((near, self_best))
    far = lax.ppermute(near, "cluster", [((c + 2) % n_cluster, c) for c in range(1, n_cluster, 2)])
    table = own[:, BODY, :PAIRS].astype(jnp.int32).reshape(-1)
    picked = pl.pallas_call(
        pick,
        in_specs=[SMEM, SMEM, VMEM, VMEM, ANY],
        out_specs=VMEM,
        scratch_shapes=[pltpu.VMEM((GROUP, TALL, LANES), jnp.bfloat16), pltpu.SemaphoreType.DMA],
        out_shape=jax.ShapeDtypeStruct((GROUP, SLOTS, BODY, LANES), jnp.bfloat16),
        compiler_params=pltpu.CompilerParams(vmem_limit_bytes=16 * 2**20),
    )(table, odd[None], own, near, far)
    picked, info, self_best, is_odd = lax.optimization_barrier((picked, info, self_best, odd == 1))
    got = exchange(picked)
    best_shape = jax.ShapeDtypeStruct((1, ROWS), jnp.float32)
    send_shape = jax.ShapeDtypeStruct((2 * GROUP, 1, ROWS), jnp.float32)
    over_shape = jax.ShapeDtypeStruct((GROUP, 1, ROWS), jnp.float32)
    params = pltpu.CompilerParams(vmem_limit_bytes=12 * 2**20)
    best, send, over = pl.pallas_call(
        even_scores,
        in_specs=[SMEM, VMEM, VMEM],
        out_specs=[VMEM] * 3,
        out_shape=[best_shape, send_shape, over_shape],
        compiler_params=params,
    )(info, unit, got)
    over = lax.ppermute(over, "cluster", [(c, c ^ 1) for c in range(n_cluster)])
    best, send = pl.pallas_call(
        odd_scores,
        in_specs=[SMEM] + [VMEM] * 5,
        out_specs=[VMEM] * 2,
        out_shape=[best_shape, send_shape],
        input_output_aliases={4: 0, 5: 1},
        compiler_params=params,
        cost_estimate=pl.CostEstimate(flops=SLOTS * 2 * ROWS * ROWS * D, bytes_accessed=4 * ROWS * D * 2, transcendentals=0),
    )(info, unit, got, self_best, best, send)
    first = jnp.where(is_odd, jnp.maximum(send[:GROUP], over), send[:GROUP])
    send = jnp.concatenate([first, send[GROUP:]])
    reach = [
        [c * GROUP + s for c in (odd_one, (odd_one + 1) % n_cluster) for s in REACH]
        for odd_one in range(1, n_cluster, 2)
    ]
    back = lax.all_to_all(send, ("cluster", "shard"), 0, 0, axis_index_groups=reach, tiled=True)
    best = jnp.maximum(best[0], jnp.max(back, axis=(0, 1)))
    return jnp.where(jnp.arange(ROWS, dtype=jnp.int32) < counts[0], best, 0.0)


def solution(mesh):
    return jax.shard_map(
        shards,
        mesh=mesh,
        in_specs=(
            P(("cluster", "shard"), None),
            P(("cluster", "shard"), None),
            P(("cluster", "shard")),
        ),
        out_specs=P(("cluster", "shard")),
        check_vma=False,
    )
```

```python
import jax
import jax.numpy as jnp
from jax import lax
from jax.experimental import pallas as pl
from jax.experimental.pallas import tpu as pltpu
from jax.sharding import PartitionSpec as P

ROWS = 512
D = 1024
PAIRS = 4
SLOTS = PAIRS - 1
GROUP = 16
CUT = ROWS // GROUP
LANES = 128
TILES = D // LANES
BODY = TILES * CUT
TALL = BODY + 16
STEP = 256
ORDER = [10, 15, 13, 11, 2, 14, 6, 7, 0, 9, 5, 4, 8, 1, 3, 12]
REACH = ORDER
PLACE = [ORDER.index(s) for s in range(GROUP)]
REACH_PLACE = [REACH.index(s) for s in range(GROUP)]
VMEM = pl.BlockSpec(memory_space=pltpu.VMEM)
SMEM = pl.BlockSpec(memory_space=pltpu.SMEM)
ANY = pl.BlockSpec(memory_space=pl.ANY)


def moved(code, places):
    shard = code % GROUP
    place = shard
    for s in range(GROUP):
        place = jnp.where(shard == s, places[s], place)
    return place + code - shard


def by_place(code):
    return moved(code, PLACE)


def to_reach(code):
    return moved(code, REACH_PLACE)


def unit_rows(raw):
    raw = raw.astype(jnp.float32)
    return raw * lax.rsqrt(jnp.sum(raw * raw, axis=1, keepdims=True) + 1e-06)


def normalise(partners_ref, counts_ref, doc_ref, unit, raw, partners, counts, in_sem, small_sem):
    small = [
        pltpu.make_async_copy(partners_ref, partners, small_sem.at[0]),
        pltpu.make_async_copy(counts_ref, counts, small_sem.at[1]),
    ]
    fetch = [
        pltpu.make_async_copy(doc_ref.at[pl.ds(i, STEP)], raw.at[pl.ds(i, STEP)], in_sem.at[i // STEP])
        for i in range(0, ROWS, STEP)
    ]
    for copy in small + fetch:
        copy.start()
    for copy in small:
        copy.wait()
    lane = lax.broadcasted_iota(jnp.int32, (16, LANES), 1)
    entry = jnp.where(lane == 0, by_place(partners[0, 0]), 0)
    for p in range(1, PAIRS):
        entry = jnp.where(lane == p, by_place(partners[0, p]), entry)
    entry = entry.astype(jnp.float32).astype(jnp.bfloat16)
    for i in range(0, ROWS, STEP):
        fetch[i // STEP].wait()
        rows = unit_rows(raw[i : i + STEP])
        if i == 0:
            first = rows[:1]
        row = i + lax.broadcasted_iota(jnp.int32, (STEP, 1), 0)
        rows = jnp.where(row < counts[0], rows, first).astype(jnp.bfloat16)
        for j in range(0, STEP, CUT):
            at = (i + j) // CUT
            for t in range(TILES):
                unit[at, t * CUT : (t + 1) * CUT] = rows[j : j + CUT, t * LANES : (t + 1) * LANES]
            unit[at, BODY:] = entry


def pick(table_ref, info_ref, own_ref, near_ref, far_ref, out_ref):
    def each(body):
        for e in range(GROUP * SLOTS):
            dst, slot = e // SLOTS, e % SLOTS
            body(dst, slot, table_ref[dst * PAIRS + 1 + slot])

    def from_own(dst, slot, code):
        @pl.when(code < GROUP)
        def _():
            out_ref[dst, slot] = own_ref[code, :BODY]

    def from_next(next_ref):
        def one(dst, slot, code):
            @pl.when(code >= GROUP)
            def _():
                out_ref[dst, slot] = next_ref[code - GROUP, :BODY]

        return one

    each(from_own)

    @pl.when(info_ref[0] == 0)
    def _():
        each(from_next(near_ref))

    @pl.when(info_ref[0] == 1)
    def _():
        each(from_next(far_ref))


def rows_of(slices):
    tiles = [slices[:, t * CUT : (t + 1) * CUT].reshape(ROWS, LANES) for t in range(TILES)]
    return jnp.concatenate(tiles, axis=1)


def products(left, right):
    return lax.dot_general(left, right, (((1,), (1,)), ((), ())), preferred_element_type=jnp.float32)


def folded(part, rows):
    for t in range(rows.shape[1] // 128):
        part = jnp.maximum(part, rows[:, t * 128 : (t + 1) * 128])
    return part


def self_part(count, unit):
    row = lax.broadcasted_iota(jnp.int32, (ROWS, 1), 0)
    col = lax.broadcasted_iota(jnp.int32, (1, ROWS), 1)
    rows = jnp.where(jnp.logical_and(col < count, row != col), products(unit, unit), -1.0)
    return folded(jnp.full((ROWS, 128), -1.0, jnp.float32), rows)


def highest(part):
    return jnp.max(part.T, axis=0, keepdims=True)


def odd_self(info_ref, unit_ref, best_ref):
    @pl.when(info_ref[0] == 1)
    def _():
        best_ref[...] = highest(self_part(info_ref[2 + PAIRS], rows_of(unit_ref)))

    @pl.when(info_ref[0] == 0)
    def _():
        best_ref[...] = jnp.full(best_ref.shape, -1.0, jnp.float32)


def pair_scores(info_ref, unit_ref, got_ref, send_ref, over_ref=None):
    odd, mine = info_ref[0], info_ref[1]
    unit = rows_of(unit_ref)
    send_ref[...] = jnp.full(send_ref.shape, -1.0, jnp.float32)
    part = jnp.full((ROWS, 128), -1.0, jnp.float32)
    for p in range(SLOTS):
        code = info_ref[3 + p]
        twice = code == mine
        scores = products(unit, rows_of(got_ref.at[:, p]))
        part = jnp.where(twice, part, folded(part, scores))
        cols = jnp.where(twice, -1.0, jnp.max(scores, axis=0, keepdims=True))
        line = to_reach(code) + jnp.where(odd == 1, 0, GROUP)

        @pl.when(line < 2 * GROUP)
        def _():
            send_ref[line] = jnp.maximum(send_ref[line], cols)

        if over_ref is not None:

            @pl.when(line >= 2 * GROUP)
            def _():
                over_ref[line - 2 * GROUP] = jnp.maximum(over_ref[line - 2 * GROUP], cols)

    return part


def even_scores(info_ref, unit_ref, got_ref, best_ref, send_ref, over_ref):
    over_ref[...] = jnp.full(over_ref.shape, -1.0, jnp.float32)

    @pl.when(info_ref[0] == 0)
    def _():
        part = pair_scores(info_ref, unit_ref, got_ref, send_ref, over_ref)
        best_ref[...] = highest(jnp.maximum(part, self_part(info_ref[2 + PAIRS], rows_of(unit_ref))))


def odd_scores(info_ref, unit_ref, got_ref, self_ref, held_best_ref, held_send_ref, best_ref, send_ref):
    @pl.when(info_ref[0] == 1)
    def _():
        part = pair_scores(info_ref, unit_ref, got_ref, send_ref)
        best_ref[...] = jnp.maximum(highest(part), self_ref[...])

    @pl.when(info_ref[0] == 0)
    def _():
        best_ref[...] = held_best_ref[...]
        send_ref[...] = held_send_ref[...]


def exchange(parts):
    return lax.all_to_all(parts, "shard", 0, 0, axis_index_groups=[ORDER], tiled=True)


def shards(documents, partners, counts):
    n_cluster = lax.axis_size("cluster")
    my_cluster, my_shard = lax.axis_index("cluster"), lax.axis_index("shard")
    odd = my_cluster % 2
    unit = pl.pallas_call(
        normalise,
        in_specs=[ANY] * 3,
        out_specs=VMEM,
        out_shape=jax.ShapeDtypeStruct((GROUP, TALL, LANES), jnp.bfloat16),
        scratch_shapes=[
            pltpu.VMEM((ROWS, D), jnp.bfloat16),
            pltpu.SMEM((1, PAIRS), jnp.int32),
            pltpu.SMEM((1,), jnp.int32),
            pltpu.SemaphoreType.DMA((ROWS // STEP,)),
            pltpu.SemaphoreType.DMA((2,)),
        ],
        compiler_params=pltpu.CompilerParams(vmem_limit_bytes=8 * 2**20),
    )(partners, counts, documents)
    own = exchange(unit)
    near = lax.ppermute(own, "cluster", [(c, c ^ 1) for c in range(n_cluster)])
    info = jnp.concatenate([odd[None], my_shard[None], partners[0], counts])
    held, own = lax.optimization_barrier((unit, own))
    self_best = pl.pallas_call(
        odd_self,
        in_specs=[SMEM, VMEM],
        out_specs=VMEM,
        out_shape=jax.ShapeDtypeStruct((1, ROWS), jnp.float32),
        cost_estimate=pl.CostEstimate(flops=2 * ROWS * ROWS * D, bytes_accessed=ROWS * D * 2, transcendentals=0),
        compiler_params=pltpu.CompilerParams(vmem_limit_bytes=12 * 2**20),
    )(info, held)
    table = own[:, BODY, :PAIRS].astype(jnp.int32).reshape(-1)
    near, self_best, table, info, is_odd = lax.optimization_barrier((near, self_best, table, info, odd == 1))
    far = lax.ppermute(near, "cluster", [((c + 2) % n_cluster, c) for c in range(1, n_cluster, 2)])
    picked = pl.pallas_call(
        pick,
        in_specs=[SMEM, SMEM, VMEM, VMEM, VMEM],
        out_specs=VMEM,
        out_shape=jax.ShapeDtypeStruct((GROUP, SLOTS, BODY, LANES), jnp.bfloat16),
        compiler_params=pltpu.CompilerParams(vmem_limit_bytes=8 * 2**20),
    )(table, info, own, near, far)
    picked, info, self_best, is_odd = lax.optimization_barrier((picked, info, self_best, is_odd))
    got = exchange(picked)
    best_shape = jax.ShapeDtypeStruct((1, ROWS), jnp.float32)
    send_shape = jax.ShapeDtypeStruct((2 * GROUP, 1, ROWS), jnp.float32)
    over_shape = jax.ShapeDtypeStruct((GROUP, 1, ROWS), jnp.float32)
    params = pltpu.CompilerParams(vmem_limit_bytes=12 * 2**20)
    best, send, over = pl.pallas_call(
        even_scores,
        in_specs=[SMEM, VMEM, VMEM],
        out_specs=[VMEM] * 3,
        out_shape=[best_shape, send_shape, over_shape],
        compiler_params=params,
    )(info, unit, got)
    over = lax.ppermute(over, "cluster", [(c, c ^ 1) for c in range(n_cluster)])
    best, send = pl.pallas_call(
        odd_scores,
        in_specs=[SMEM] + [VMEM] * 5,
        out_specs=[VMEM] * 2,
        out_shape=[best_shape, send_shape],
        input_output_aliases={4: 0, 5: 1},
        compiler_params=params,
        cost_estimate=pl.CostEstimate(flops=SLOTS * 2 * ROWS * ROWS * D, bytes_accessed=4 * ROWS * D * 2, transcendentals=0),
    )(info, unit, got, self_best, best, send)
    first = jnp.where(is_odd, jnp.maximum(send[:GROUP], over), send[:GROUP])
    send = jnp.concatenate([first, send[GROUP:]])
    reach = [
        [c * GROUP + s for c in (odd_one, (odd_one + 1) % n_cluster) for s in REACH]
        for odd_one in range(1, n_cluster, 2)
    ]
    back = lax.all_to_all(send, ("cluster", "shard"), 0, 0, axis_index_groups=reach, tiled=True)
    best = jnp.maximum(best[0], jnp.max(back, axis=(0, 1)))
    return jnp.where(jnp.arange(ROWS, dtype=jnp.int32) < counts[0], best, 0.0)


def solution(mesh):
    return jax.shard_map(
        shards,
        mesh=mesh,
        in_specs=(
            P(("cluster", "shard"), None),
            P(("cluster", "shard"), None),
            P(("cluster", "shard")),
        ),
        out_specs=P(("cluster", "shard")),
        check_vma=False,
    )
```

```python
import jax
import jax.numpy as jnp
from jax import lax
from jax.experimental import pallas as pl
from jax.experimental.pallas import tpu as pltpu
from jax.sharding import PartitionSpec as P

ROWS = 512
D = 1024
PAIRS = 4
SLOTS = PAIRS - 1
GROUP = 16
CUT = ROWS // GROUP
LANES = 128
TILES = D // LANES
BODY = TILES * CUT
TALL = BODY + 16
STEP = 256
ORDER = [10, 15, 13, 11, 12, 14, 6, 7, 0, 9, 5, 4, 8, 1, 3, 2]
REACH = [10, 15, 13, 11, 2, 14, 6, 7, 0, 9, 5, 4, 8, 1, 3, 12]
PLACE = [ORDER.index(s) for s in range(GROUP)]
REACH_PLACE = [REACH.index(s) for s in range(GROUP)]
VMEM = pl.BlockSpec(memory_space=pltpu.VMEM)
SMEM = pl.BlockSpec(memory_space=pltpu.SMEM)
ANY = pl.BlockSpec(memory_space=pl.ANY)


def moved(code, places):
    shard = code % GROUP
    place = shard
    for s in range(GROUP):
        place = jnp.where(shard == s, places[s], place)
    return place + code - shard


def by_place(code):
    return moved(code, PLACE)


def to_reach(code):
    return moved(code, REACH_PLACE)


def unit_rows(raw):
    raw = raw.astype(jnp.float32)
    return raw * lax.rsqrt(jnp.sum(raw * raw, axis=1, keepdims=True) + 1e-06)


def normalise(partners_ref, counts_ref, doc_ref, unit, raw, partners, counts, in_sem, small_sem):
    small = [
        pltpu.make_async_copy(partners_ref, partners, small_sem.at[0]),
        pltpu.make_async_copy(counts_ref, counts, small_sem.at[1]),
    ]
    fetch = [
        pltpu.make_async_copy(doc_ref.at[pl.ds(i, STEP)], raw.at[pl.ds(i, STEP)], in_sem.at[i // STEP])
        for i in range(0, ROWS, STEP)
    ]
    for copy in small + fetch:
        copy.start()
    for copy in small:
        copy.wait()
    lane = lax.broadcasted_iota(jnp.int32, (16, LANES), 1)
    entry = jnp.where(lane == 0, by_place(partners[0, 0]), 0)
    for p in range(1, PAIRS):
        entry = jnp.where(lane == p, by_place(partners[0, p]), entry)
    entry = entry.astype(jnp.float32).astype(jnp.bfloat16)
    for i in range(0, ROWS, STEP):
        fetch[i // STEP].wait()
        rows = unit_rows(raw[i : i + STEP])
        if i == 0:
            first = rows[:1]
        row = i + lax.broadcasted_iota(jnp.int32, (STEP, 1), 0)
        rows = jnp.where(row < counts[0], rows, first).astype(jnp.bfloat16)
        for j in range(0, STEP, CUT):
            at = (i + j) // CUT
            for t in range(TILES):
                unit[at, t * CUT : (t + 1) * CUT] = rows[j : j + CUT, t * LANES : (t + 1) * LANES]
            unit[at, BODY:] = entry


def pick(table_ref, info_ref, own_ref, near_ref, far_ref, out_ref):
    def all_from(next_ref):
        for e in range(GROUP * SLOTS):
            dst, slot = e // SLOTS, e % SLOTS
            code = table_ref[dst * PAIRS + 1 + slot]

            @pl.when(code < GROUP)
            def _():
                out_ref[dst, slot] = own_ref[code, :BODY]

            @pl.when(code >= GROUP)
            def _():
                out_ref[dst, slot] = next_ref[code - GROUP, :BODY]

    @pl.when(info_ref[0] == 0)
    def _():
        all_from(near_ref)

    @pl.when(info_ref[0] == 1)
    def _():
        all_from(far_ref)


def rows_of(slices):
    tiles = [slices[:, t * CUT : (t + 1) * CUT].reshape(ROWS, LANES) for t in range(TILES)]
    return jnp.concatenate(tiles, axis=1)


def products(left, right):
    return lax.dot_general(left, right, (((1,), (1,)), ((), ())), preferred_element_type=jnp.float32)


def folded(part, rows):
    for t in range(rows.shape[1] // 128):
        part = jnp.maximum(part, rows[:, t * 128 : (t + 1) * 128])
    return part


def self_part(count, unit):
    row = lax.broadcasted_iota(jnp.int32, (ROWS, 1), 0)
    col = lax.broadcasted_iota(jnp.int32, (1, ROWS), 1)
    rows = jnp.where(jnp.logical_and(col < count, row != col), products(unit, unit), -1.0)
    return folded(jnp.full((ROWS, 128), -1.0, jnp.float32), rows)


def highest(part):
    return jnp.max(part.T, axis=0, keepdims=True)


def odd_self(info_ref, unit_ref, best_ref):
    @pl.when(info_ref[0] == 1)
    def _():
        best_ref[...] = highest(self_part(info_ref[2 + PAIRS], rows_of(unit_ref)))

    @pl.when(info_ref[0] == 0)
    def _():
        best_ref[...] = jnp.full(best_ref.shape, -1.0, jnp.float32)


def pair_scores(info_ref, unit_ref, got_ref, send_ref, over_ref=None):
    odd, mine = info_ref[0], info_ref[1]
    unit = rows_of(unit_ref)
    send_ref[...] = jnp.full(send_ref.shape, -1.0, jnp.float32)
    part = jnp.full((ROWS, 128), -1.0, jnp.float32)
    for p in range(SLOTS):
        code = info_ref[3 + p]
        twice = code == mine
        scores = products(unit, rows_of(got_ref.at[:, p]))
        part = jnp.where(twice, part, folded(part, scores))
        cols = jnp.where(twice, -1.0, jnp.max(scores, axis=0, keepdims=True))
        line = to_reach(code) + jnp.where(odd == 1, 0, GROUP)

        @pl.when(line < 2 * GROUP)
        def _():
            send_ref[line] = jnp.maximum(send_ref[line], cols)

        if over_ref is not None:

            @pl.when(line >= 2 * GROUP)
            def _():
                over_ref[line - 2 * GROUP] = jnp.maximum(over_ref[line - 2 * GROUP], cols)

    return part


def even_scores(info_ref, unit_ref, got_ref, best_ref, send_ref, over_ref):
    over_ref[...] = jnp.full(over_ref.shape, -1.0, jnp.float32)

    @pl.when(info_ref[0] == 0)
    def _():
        part = pair_scores(info_ref, unit_ref, got_ref, send_ref, over_ref)
        best_ref[...] = highest(jnp.maximum(part, self_part(info_ref[2 + PAIRS], rows_of(unit_ref))))


def odd_scores(info_ref, unit_ref, got_ref, self_ref, held_best_ref, held_send_ref, best_ref, send_ref):
    @pl.when(info_ref[0] == 1)
    def _():
        part = pair_scores(info_ref, unit_ref, got_ref, send_ref)
        best_ref[...] = jnp.maximum(highest(part), self_ref[...])

    @pl.when(info_ref[0] == 0)
    def _():
        best_ref[...] = held_best_ref[...]
        send_ref[...] = held_send_ref[...]


def exchange(parts):
    return lax.all_to_all(parts, "shard", 0, 0, axis_index_groups=[ORDER], tiled=True)


def shards(documents, partners, counts):
    n_cluster = lax.axis_size("cluster")
    my_cluster, my_shard = lax.axis_index("cluster"), lax.axis_index("shard")
    odd = my_cluster % 2
    unit = pl.pallas_call(
        normalise,
        in_specs=[ANY] * 3,
        out_specs=VMEM,
        out_shape=jax.ShapeDtypeStruct((GROUP, TALL, LANES), jnp.bfloat16),
        scratch_shapes=[
            pltpu.VMEM((ROWS, D), jnp.bfloat16),
            pltpu.SMEM((1, PAIRS), jnp.int32),
            pltpu.SMEM((1,), jnp.int32),
            pltpu.SemaphoreType.DMA((ROWS // STEP,)),
            pltpu.SemaphoreType.DMA((2,)),
        ],
        compiler_params=pltpu.CompilerParams(vmem_limit_bytes=8 * 2**20),
    )(partners, counts, documents)
    own = exchange(unit)
    near = lax.ppermute(own, "cluster", [(c, c ^ 1) for c in range(n_cluster)])
    info = jnp.concatenate([odd[None], my_shard[None], partners[0], counts])
    held, own = lax.optimization_barrier((unit, own))
    self_best = pl.pallas_call(
        odd_self,
        in_specs=[SMEM, VMEM],
        out_specs=VMEM,
        out_shape=jax.ShapeDtypeStruct((1, ROWS), jnp.float32),
        cost_estimate=pl.CostEstimate(flops=2 * ROWS * ROWS * D, bytes_accessed=ROWS * D * 2, transcendentals=0),
        compiler_params=pltpu.CompilerParams(vmem_limit_bytes=12 * 2**20),
    )(info, held)
    table = own[:, BODY, :PAIRS].astype(jnp.int32).reshape(-1)
    near, self_best, table, info, is_odd = lax.optimization_barrier((near, self_best, table, info, odd == 1))
    far = lax.ppermute(near, "cluster", [((c + 2) % n_cluster, c) for c in range(1, n_cluster, 2)])
    picked = pl.pallas_call(
        pick,
        in_specs=[SMEM, SMEM, VMEM, VMEM, VMEM],
        out_specs=VMEM,
        out_shape=jax.ShapeDtypeStruct((GROUP, SLOTS, BODY, LANES), jnp.bfloat16),
        compiler_params=pltpu.CompilerParams(vmem_limit_bytes=8 * 2**20),
    )(table, info, own, near, far)
    picked, info, self_best, is_odd = lax.optimization_barrier((picked, info, self_best, is_odd))
    got = exchange(picked)
    best_shape = jax.ShapeDtypeStruct((1, ROWS), jnp.float32)
    send_shape = jax.ShapeDtypeStruct((2 * GROUP, 1, ROWS), jnp.float32)
    over_shape = jax.ShapeDtypeStruct((GROUP, 1, ROWS), jnp.float32)
    params = pltpu.CompilerParams(vmem_limit_bytes=12 * 2**20)
    best, send, over = pl.pallas_call(
        even_scores,
        in_specs=[SMEM, VMEM, VMEM],
        out_specs=[VMEM] * 3,
        out_shape=[best_shape, send_shape, over_shape],
        compiler_params=params,
    )(info, unit, got)
    over = lax.ppermute(over, "cluster", [(c, c ^ 1) for c in range(n_cluster)])
    best, send = pl.pallas_call(
        odd_scores,
        in_specs=[SMEM] + [VMEM] * 5,
        out_specs=[VMEM] * 2,
        out_shape=[best_shape, send_shape],
        input_output_aliases={4: 0, 5: 1},
        compiler_params=params,
        cost_estimate=pl.CostEstimate(flops=SLOTS * 2 * ROWS * ROWS * D, bytes_accessed=4 * ROWS * D * 2, transcendentals=0),
    )(info, unit, got, self_best, best, send)
    first = jnp.where(is_odd, jnp.maximum(send[:GROUP], over), send[:GROUP])
    send = jnp.concatenate([first, send[GROUP:]])
    reach = [
        [c * GROUP + s for c in (odd_one, (odd_one + 1) % n_cluster) for s in REACH]
        for odd_one in range(1, n_cluster, 2)
    ]
    back = lax.all_to_all(send, ("cluster", "shard"), 0, 0, axis_index_groups=reach, tiled=True)
    best = jnp.maximum(best[0], jnp.max(back, axis=(0, 1)))
    return jnp.where(jnp.arange(ROWS, dtype=jnp.int32) < counts[0], best, 0.0)


def solution(mesh):
    return jax.shard_map(
        shards,
        mesh=mesh,
        in_specs=(
            P(("cluster", "shard"), None),
            P(("cluster", "shard"), None),
            P(("cluster", "shard")),
        ),
        out_specs=P(("cluster", "shard")),
        check_vma=False,
    )
```

```python
import jax
import jax.numpy as jnp
from jax import lax
from jax.experimental import pallas as pl
from jax.experimental.pallas import tpu as pltpu
from jax.sharding import PartitionSpec as P

ROWS = 512
D = 1024
PAIRS = 4
SLOTS = PAIRS - 1
GROUP = 16
CUT = ROWS // GROUP
LANES = 128
TILES = D // LANES
BODY = TILES * CUT
TALL = BODY + 8
STEP = 256
ORDER = [10, 15, 13, 11, 12, 14, 6, 7, 0, 9, 5, 4, 8, 1, 3, 2]
REACH = [10, 15, 13, 11, 2, 14, 6, 7, 0, 9, 5, 4, 8, 1, 3, 12]
PLACE = [ORDER.index(s) for s in range(GROUP)]
REACH_PLACE = [REACH.index(s) for s in range(GROUP)]
VMEM = pl.BlockSpec(memory_space=pltpu.VMEM)
SMEM = pl.BlockSpec(memory_space=pltpu.SMEM)
ANY = pl.BlockSpec(memory_space=pl.ANY)


def moved(code, places):
    shard = code % GROUP
    place = shard
    for s in range(GROUP):
        place = jnp.where(shard == s, places[s], place)
    return place + code - shard


def by_place(code):
    return moved(code, PLACE)


def to_reach(code):
    return moved(code, REACH_PLACE)


def unit_rows(raw):
    raw = raw.astype(jnp.float32)
    return raw * lax.rsqrt(jnp.sum(raw * raw, axis=1, keepdims=True) + 1e-06)


def normalise(partners_ref, counts_ref, doc_ref, unit, raw, partners, counts, in_sem, small_sem):
    small = [
        pltpu.make_async_copy(partners_ref, partners, small_sem.at[0]),
        pltpu.make_async_copy(counts_ref, counts, small_sem.at[1]),
    ]
    fetch = [
        pltpu.make_async_copy(doc_ref.at[pl.ds(i, STEP)], raw.at[pl.ds(i, STEP)], in_sem.at[i // STEP])
        for i in range(0, ROWS, STEP)
    ]
    for copy in small + fetch:
        copy.start()
    for copy in small:
        copy.wait()
    lane = lax.broadcasted_iota(jnp.int32, (TALL - BODY, LANES), 1)
    entry = jnp.where(lane == 0, by_place(partners[0, 0]), 0)
    for p in range(1, PAIRS):
        entry = jnp.where(lane == p, by_place(partners[0, p]), entry)
    entry = entry.astype(jnp.float32).astype(jnp.bfloat16)
    for i in range(0, ROWS, STEP):
        fetch[i // STEP].wait()
        rows = unit_rows(raw[i : i + STEP])
        if i == 0:
            first = rows[:1]
        row = i + lax.broadcasted_iota(jnp.int32, (STEP, 1), 0)
        rows = jnp.where(row < counts[0], rows, first).astype(jnp.bfloat16)
        for j in range(0, STEP, CUT):
            at = (i + j) // CUT
            for t in range(TILES):
                unit[at, t * CUT : (t + 1) * CUT] = rows[j : j + CUT, t * LANES : (t + 1) * LANES]
            unit[at, BODY:] = entry


def pick(table_ref, info_ref, own_ref, near_ref, far_ref, out_ref):
    def all_from(next_ref):
        for e in range(GROUP * SLOTS):
            dst, slot = e // SLOTS, e % SLOTS
            code = table_ref[dst * PAIRS + 1 + slot]

            @pl.when(code < GROUP)
            def _():
                out_ref[dst, slot] = own_ref[code, :BODY]

            @pl.when(code >= GROUP)
            def _():
                out_ref[dst, slot] = next_ref[code - GROUP, :BODY]

    @pl.when(info_ref[0] == 0)
    def _():
        all_from(near_ref)

    @pl.when(info_ref[0] == 1)
    def _():
        all_from(far_ref)


def rows_of(slices):
    tiles = [slices[:, t * CUT : (t + 1) * CUT].reshape(ROWS, LANES) for t in range(TILES)]
    return jnp.concatenate(tiles, axis=1)


def products(left, right):
    return lax.dot_general(left, right, (((1,), (1,)), ((), ())), preferred_element_type=jnp.float32)


def folded(part, rows):
    for t in range(rows.shape[1] // 128):
        part = jnp.maximum(part, rows[:, t * 128 : (t + 1) * 128])
    return part


def self_part(count, unit):
    row = lax.broadcasted_iota(jnp.int32, (ROWS, 1), 0)
    col = lax.broadcasted_iota(jnp.int32, (1, ROWS), 1)
    rows = jnp.where(jnp.logical_and(col < count, row != col), products(unit, unit), -1.0)
    return folded(jnp.full((ROWS, 128), -1.0, jnp.float32), rows)


def highest(part):
    return jnp.max(part.T, axis=0, keepdims=True)


def odd_self(info_ref, unit_ref, best_ref):
    @pl.when(info_ref[0] == 1)
    def _():
        best_ref[...] = highest(self_part(info_ref[2 + PAIRS], rows_of(unit_ref)))

    @pl.when(info_ref[0] == 0)
    def _():
        best_ref[...] = jnp.full(best_ref.shape, -1.0, jnp.float32)


def pair_scores(info_ref, unit_ref, got_ref, send_ref, over_ref=None):
    odd, mine = info_ref[0], info_ref[1]
    unit = rows_of(unit_ref)
    send_ref[...] = jnp.full(send_ref.shape, -1.0, jnp.float32)
    part = jnp.full((ROWS, 128), -1.0, jnp.float32)
    for p in range(SLOTS):
        code = info_ref[3 + p]
        twice = code == mine
        scores = products(unit, rows_of(got_ref.at[:, p]))
        part = jnp.where(twice, part, folded(part, scores))
        cols = jnp.where(twice, -1.0, jnp.max(scores, axis=0, keepdims=True))
        line = to_reach(code) + jnp.where(odd == 1, 0, GROUP)

        @pl.when(line < 2 * GROUP)
        def _():
            send_ref[line] = jnp.maximum(send_ref[line], cols)

        if over_ref is not None:

            @pl.when(line >= 2 * GROUP)
            def _():
                over_ref[line - 2 * GROUP] = jnp.maximum(over_ref[line - 2 * GROUP], cols)

    return part


def even_scores(info_ref, unit_ref, got_ref, best_ref, send_ref, over_ref):
    over_ref[...] = jnp.full(over_ref.shape, -1.0, jnp.float32)

    @pl.when(info_ref[0] == 0)
    def _():
        part = pair_scores(info_ref, unit_ref, got_ref, send_ref, over_ref)
        best_ref[...] = highest(jnp.maximum(part, self_part(info_ref[2 + PAIRS], rows_of(unit_ref))))


def odd_scores(info_ref, unit_ref, got_ref, self_ref, held_best_ref, held_send_ref, best_ref, send_ref):
    @pl.when(info_ref[0] == 1)
    def _():
        part = pair_scores(info_ref, unit_ref, got_ref, send_ref)
        best_ref[...] = jnp.maximum(highest(part), self_ref[...])

    @pl.when(info_ref[0] == 0)
    def _():
        best_ref[...] = held_best_ref[...]
        send_ref[...] = held_send_ref[...]


def exchange(parts):
    return lax.all_to_all(parts, "shard", 0, 0, axis_index_groups=[ORDER], tiled=True)


def shards(documents, partners, counts):
    n_cluster = lax.axis_size("cluster")
    my_cluster, my_shard = lax.axis_index("cluster"), lax.axis_index("shard")
    odd = my_cluster % 2
    unit = pl.pallas_call(
        normalise,
        in_specs=[ANY] * 3,
        out_specs=VMEM,
        out_shape=jax.ShapeDtypeStruct((GROUP, TALL, LANES), jnp.bfloat16),
        scratch_shapes=[
            pltpu.VMEM((ROWS, D), jnp.bfloat16),
            pltpu.SMEM((1, PAIRS), jnp.int32),
            pltpu.SMEM((1,), jnp.int32),
            pltpu.SemaphoreType.DMA((ROWS // STEP,)),
            pltpu.SemaphoreType.DMA((2,)),
        ],
        compiler_params=pltpu.CompilerParams(vmem_limit_bytes=8 * 2**20),
    )(partners, counts, documents)
    own = exchange(unit)
    near = lax.ppermute(own, "cluster", [(c, c ^ 1) for c in range(n_cluster)])
    info = jnp.concatenate([odd[None], my_shard[None], partners[0], counts])
    held, own = lax.optimization_barrier((unit, own))
    self_best = pl.pallas_call(
        odd_self,
        in_specs=[SMEM, VMEM],
        out_specs=VMEM,
        out_shape=jax.ShapeDtypeStruct((1, ROWS), jnp.float32),
        cost_estimate=pl.CostEstimate(flops=2 * ROWS * ROWS * D, bytes_accessed=ROWS * D * 2, transcendentals=0),
        compiler_params=pltpu.CompilerParams(vmem_limit_bytes=12 * 2**20),
    )(info, held)
    table = own[:, BODY, :PAIRS].astype(jnp.int32).reshape(-1)
    near, self_best, table, info, is_odd = lax.optimization_barrier((near, self_best, table, info, odd == 1))
    far = lax.ppermute(near, "cluster", [((c + 2) % n_cluster, c) for c in range(1, n_cluster, 2)])
    picked = pl.pallas_call(
        pick,
        in_specs=[SMEM, SMEM, VMEM, VMEM, VMEM],
        out_specs=VMEM,
        out_shape=jax.ShapeDtypeStruct((GROUP, SLOTS, BODY, LANES), jnp.bfloat16),
        compiler_params=pltpu.CompilerParams(vmem_limit_bytes=8 * 2**20),
    )(table, info, own, near, far)
    picked, info, self_best, is_odd = lax.optimization_barrier((picked, info, self_best, is_odd))
    got = exchange(picked)
    best_shape = jax.ShapeDtypeStruct((1, ROWS), jnp.float32)
    send_shape = jax.ShapeDtypeStruct((2 * GROUP, 1, ROWS), jnp.float32)
    over_shape = jax.ShapeDtypeStruct((GROUP, 1, ROWS), jnp.float32)
    params = pltpu.CompilerParams(vmem_limit_bytes=12 * 2**20)
    best, send, over = pl.pallas_call(
        even_scores,
        in_specs=[SMEM, VMEM, VMEM],
        out_specs=[VMEM] * 3,
        out_shape=[best_shape, send_shape, over_shape],
        compiler_params=params,
    )(info, unit, got)
    over = lax.ppermute(over, "cluster", [(c, c ^ 1) for c in range(n_cluster)])
    best, send = pl.pallas_call(
        odd_scores,
        in_specs=[SMEM] + [VMEM] * 5,
        out_specs=[VMEM] * 2,
        out_shape=[best_shape, send_shape],
        input_output_aliases={4: 0, 5: 1},
        compiler_params=params,
        cost_estimate=pl.CostEstimate(flops=SLOTS * 2 * ROWS * ROWS * D, bytes_accessed=4 * ROWS * D * 2, transcendentals=0),
    )(info, unit, got, self_best, best, send)
    first = jnp.where(is_odd, jnp.maximum(send[:GROUP], over), send[:GROUP])
    send = jnp.concatenate([first, send[GROUP:]])
    reach = [
        [c * GROUP + s for c in (odd_one, (odd_one + 1) % n_cluster) for s in REACH]
        for odd_one in range(1, n_cluster, 2)
    ]
    back = lax.all_to_all(send, ("cluster", "shard"), 0, 0, axis_index_groups=reach, tiled=True)
    best = jnp.maximum(best[0], jnp.max(back, axis=(0, 1)))
    return jnp.where(jnp.arange(ROWS, dtype=jnp.int32) < counts[0], best, 0.0)


def solution(mesh):
    return jax.shard_map(
        shards,
        mesh=mesh,
        in_specs=(
            P(("cluster", "shard"), None),
            P(("cluster", "shard"), None),
            P(("cluster", "shard")),
        ),
        out_specs=P(("cluster", "shard")),
        check_vma=False,
    )
```

```python
import jax
import jax.numpy as jnp
from jax import lax
from jax.experimental import pallas as pl
from jax.experimental.pallas import tpu as pltpu
from jax.sharding import PartitionSpec as P

ROWS = 512
D = 1024
PAIRS = 4
SLOTS = PAIRS - 1
GROUP = 16
CUT = ROWS // GROUP
LANES = 128
TILES = D // LANES
BODY = TILES * CUT
LIST = 8
TALL = BODY + LIST
STEP = 256
ORDER = [10, 15, 13, 11, 12, 14, 6, 7, 0, 9, 5, 4, 8, 1, 3, 2]
REACH = [10, 15, 13, 11, 2, 14, 6, 7, 0, 9, 5, 4, 8, 1, 3, 12]
PLACE = [ORDER.index(s) for s in range(GROUP)]
REACH_PLACE = [REACH.index(s) for s in range(GROUP)]
VMEM = pl.BlockSpec(memory_space=pltpu.VMEM)
SMEM = pl.BlockSpec(memory_space=pltpu.SMEM)
ANY = pl.BlockSpec(memory_space=pl.ANY)


def moved(code, places):
    shard = code % GROUP
    place = shard
    for s in range(GROUP):
        place = jnp.where(shard == s, places[s], place)
    return place + code - shard


def by_place(code):
    return moved(code, PLACE)


def to_reach(code):
    return moved(code, REACH_PLACE)


def unit_rows(raw):
    raw = raw.astype(jnp.float32)
    return raw * lax.rsqrt(jnp.sum(raw * raw, axis=1, keepdims=True) + 1e-06)


def normalise(partners_ref, counts_ref, doc_ref, unit, raw, partners, counts, in_sem, small_sem):
    small = [
        pltpu.make_async_copy(partners_ref, partners, small_sem.at[0]),
        pltpu.make_async_copy(counts_ref, counts, small_sem.at[1]),
    ]
    fetch = [
        pltpu.make_async_copy(doc_ref.at[pl.ds(i, STEP)], raw.at[pl.ds(i, STEP)], in_sem.at[i // STEP])
        for i in range(0, ROWS, STEP)
    ]
    for copy in small + fetch:
        copy.start()
    for copy in small:
        copy.wait()
    lane = lax.broadcasted_iota(jnp.int32, (LIST, LANES), 1)
    entry = jnp.where(lane == 0, by_place(partners[0, 0]), 0)
    for p in range(1, PAIRS):
        entry = jnp.where(lane == p, by_place(partners[0, p]), entry)
    entry = entry.astype(jnp.float32).astype(jnp.bfloat16)
    for i in range(0, ROWS, STEP):
        fetch[i // STEP].wait()
        rows = unit_rows(raw[i : i + STEP])
        if i == 0:
            first = rows[:1]
        row = i + lax.broadcasted_iota(jnp.int32, (STEP, 1), 0)
        rows = jnp.where(row < counts[0], rows, first).astype(jnp.bfloat16)
        for j in range(0, STEP, CUT):
            at = (i + j) // CUT
            for t in range(TILES):
                unit[at, t * CUT : (t + 1) * CUT] = rows[j : j + CUT, t * LANES : (t + 1) * LANES]
            last = rows[j + CUT - (16 - LIST) : j + CUT, D - LANES :]
            unit[at, TALL - 16 :] = jnp.concatenate([last, entry])


def pick(table_ref, info_ref, own_ref, near_ref, far_ref, out_ref):
    def all_from(next_ref):
        for e in range(GROUP * SLOTS):
            dst, slot = e // SLOTS, e % SLOTS
            code = table_ref[dst * PAIRS + 1 + slot]

            @pl.when(code < GROUP)
            def _():
                out_ref[dst, slot] = own_ref[code, :BODY]

            @pl.when(code >= GROUP)
            def _():
                out_ref[dst, slot] = next_ref[code - GROUP, :BODY]

    @pl.when(info_ref[0] == 0)
    def _():
        all_from(near_ref)

    @pl.when(info_ref[0] == 1)
    def _():
        all_from(far_ref)


def rows_of(slices):
    tiles = [slices[:, t * CUT : (t + 1) * CUT].reshape(ROWS, LANES) for t in range(TILES)]
    return jnp.concatenate(tiles, axis=1)


def products(left, right):
    return lax.dot_general(left, right, (((1,), (1,)), ((), ())), preferred_element_type=jnp.float32)


def folded(part, rows):
    for t in range(rows.shape[1] // 128):
        part = jnp.maximum(part, rows[:, t * 128 : (t + 1) * 128])
    return part


def self_part(count, unit):
    row = lax.broadcasted_iota(jnp.int32, (ROWS, 1), 0)
    col = lax.broadcasted_iota(jnp.int32, (1, ROWS), 1)
    rows = jnp.where(jnp.logical_and(col < count, row != col), products(unit, unit), -1.0)
    return folded(jnp.full((ROWS, 128), -1.0, jnp.float32), rows)


def highest(part):
    return jnp.max(part.T, axis=0, keepdims=True)


def odd_self(info_ref, unit_ref, best_ref):
    @pl.when(info_ref[0] == 1)
    def _():
        best_ref[...] = highest(self_part(info_ref[2 + PAIRS], rows_of(unit_ref)))

    @pl.when(info_ref[0] == 0)
    def _():
        best_ref[...] = jnp.full(best_ref.shape, -1.0, jnp.float32)


def pair_scores(info_ref, unit_ref, got_ref, send_ref, over_ref=None):
    odd, mine = info_ref[0], info_ref[1]
    unit = rows_of(unit_ref)
    send_ref[...] = jnp.full(send_ref.shape, -1.0, jnp.float32)
    part = jnp.full((ROWS, 128), -1.0, jnp.float32)
    for p in range(SLOTS):
        code = info_ref[3 + p]
        twice = code == mine
        scores = products(unit, rows_of(got_ref.at[:, p]))
        part = jnp.where(twice, part, folded(part, scores))
        cols = jnp.where(twice, -1.0, jnp.max(scores, axis=0, keepdims=True))
        line = to_reach(code) + jnp.where(odd == 1, 0, GROUP)

        @pl.when(line < 2 * GROUP)
        def _():
            send_ref[line] = jnp.maximum(send_ref[line], cols)

        if over_ref is not None:

            @pl.when(line >= 2 * GROUP)
            def _():
                over_ref[line - 2 * GROUP] = jnp.maximum(over_ref[line - 2 * GROUP], cols)

    return part


def even_scores(info_ref, unit_ref, got_ref, best_ref, send_ref, over_ref):
    over_ref[...] = jnp.full(over_ref.shape, -1.0, jnp.float32)

    @pl.when(info_ref[0] == 0)
    def _():
        part = pair_scores(info_ref, unit_ref, got_ref, send_ref, over_ref)
        best_ref[...] = highest(jnp.maximum(part, self_part(info_ref[2 + PAIRS], rows_of(unit_ref))))


def odd_scores(info_ref, unit_ref, got_ref, self_ref, held_best_ref, held_send_ref, best_ref, send_ref):
    @pl.when(info_ref[0] == 1)
    def _():
        part = pair_scores(info_ref, unit_ref, got_ref, send_ref)
        best_ref[...] = jnp.maximum(highest(part), self_ref[...])

    @pl.when(info_ref[0] == 0)
    def _():
        best_ref[...] = held_best_ref[...]
        send_ref[...] = held_send_ref[...]


def exchange(parts):
    return lax.all_to_all(parts, "shard", 0, 0, axis_index_groups=[ORDER], tiled=True)


def shards(documents, partners, counts):
    n_cluster = lax.axis_size("cluster")
    my_cluster, my_shard = lax.axis_index("cluster"), lax.axis_index("shard")
    odd = my_cluster % 2
    unit = pl.pallas_call(
        normalise,
        in_specs=[ANY] * 3,
        out_specs=VMEM,
        out_shape=jax.ShapeDtypeStruct((GROUP, TALL, LANES), jnp.bfloat16),
        scratch_shapes=[
            pltpu.VMEM((ROWS, D), jnp.bfloat16),
            pltpu.SMEM((1, PAIRS), jnp.int32),
            pltpu.SMEM((1,), jnp.int32),
            pltpu.SemaphoreType.DMA((ROWS // STEP,)),
            pltpu.SemaphoreType.DMA((2,)),
        ],
        compiler_params=pltpu.CompilerParams(vmem_limit_bytes=8 * 2**20),
    )(partners, counts, documents)
    own = exchange(unit)
    near = lax.ppermute(own, "cluster", [(c, c ^ 1) for c in range(n_cluster)])
    info = jnp.concatenate([odd[None], my_shard[None], partners[0], counts])
    held, own = lax.optimization_barrier((unit, own))
    self_best = pl.pallas_call(
        odd_self,
        in_specs=[SMEM, VMEM],
        out_specs=VMEM,
        out_shape=jax.ShapeDtypeStruct((1, ROWS), jnp.float32),
        cost_estimate=pl.CostEstimate(flops=2 * ROWS * ROWS * D, bytes_accessed=ROWS * D * 2, transcendentals=0),
        compiler_params=pltpu.CompilerParams(vmem_limit_bytes=12 * 2**20),
    )(info, held)
    table = own[:, BODY, :PAIRS].astype(jnp.int32).reshape(-1)
    near, self_best, table, info, is_odd = lax.optimization_barrier((near, self_best, table, info, odd == 1))
    far = lax.ppermute(near, "cluster", [((c + 2) % n_cluster, c) for c in range(1, n_cluster, 2)])
    picked = pl.pallas_call(
        pick,
        in_specs=[SMEM, SMEM, VMEM, VMEM, VMEM],
        out_specs=VMEM,
        out_shape=jax.ShapeDtypeStruct((GROUP, SLOTS, BODY, LANES), jnp.bfloat16),
        compiler_params=pltpu.CompilerParams(vmem_limit_bytes=8 * 2**20),
    )(table, info, own, near, far)
    picked, info, self_best, is_odd = lax.optimization_barrier((picked, info, self_best, is_odd))
    got = exchange(picked)
    best_shape = jax.ShapeDtypeStruct((1, ROWS), jnp.float32)
    send_shape = jax.ShapeDtypeStruct((2 * GROUP, 1, ROWS), jnp.float32)
    over_shape = jax.ShapeDtypeStruct((GROUP, 1, ROWS), jnp.float32)
    params = pltpu.CompilerParams(vmem_limit_bytes=12 * 2**20)
    best, send, over = pl.pallas_call(
        even_scores,
        in_specs=[SMEM, VMEM, VMEM],
        out_specs=[VMEM] * 3,
        out_shape=[best_shape, send_shape, over_shape],
        compiler_params=params,
    )(info, unit, got)
    over = lax.ppermute(over, "cluster", [(c, c ^ 1) for c in range(n_cluster)])
    best, send = pl.pallas_call(
        odd_scores,
        in_specs=[SMEM] + [VMEM] * 5,
        out_specs=[VMEM] * 2,
        out_shape=[best_shape, send_shape],
        input_output_aliases={4: 0, 5: 1},
        compiler_params=params,
        cost_estimate=pl.CostEstimate(flops=SLOTS * 2 * ROWS * ROWS * D, bytes_accessed=4 * ROWS * D * 2, transcendentals=0),
    )(info, unit, got, self_best, best, send)
    first = jnp.where(is_odd, jnp.maximum(send[:GROUP], over), send[:GROUP])
    send = jnp.concatenate([first, send[GROUP:]])
    reach = [
        [c * GROUP + s for c in (odd_one, (odd_one + 1) % n_cluster) for s in REACH]
        for odd_one in range(1, n_cluster, 2)
    ]
    back = lax.all_to_all(send, ("cluster", "shard"), 0, 0, axis_index_groups=reach, tiled=True)
    best = jnp.maximum(best[0], jnp.max(back, axis=(0, 1)))
    return jnp.where(jnp.arange(ROWS, dtype=jnp.int32) < counts[0], best, 0.0)


def solution(mesh):
    return jax.shard_map(
        shards,
        mesh=mesh,
        in_specs=(
            P(("cluster", "shard"), None),
            P(("cluster", "shard"), None),
            P(("cluster", "shard")),
        ),
        out_specs=P(("cluster", "shard")),
        check_vma=False,
    )
```

```python
import jax
import jax.numpy as jnp
from jax import lax
from jax.experimental import pallas as pl
from jax.experimental.pallas import tpu as pltpu
from jax.sharding import PartitionSpec as P

ROWS = 512
D = 1024
PAIRS = 4
SLOTS = PAIRS - 1
GROUP = 16
CUT = ROWS // GROUP
LANES = 128
TILES = D // LANES
BODY = TILES * CUT
LIST = 8
TALL = BODY + LIST
STEP = 256
ORDER = [10, 15, 13, 11, 12, 14, 6, 7, 0, 9, 5, 4, 8, 1, 3, 2]
REACH = [10, 15, 13, 11, 2, 14, 6, 7, 0, 9, 5, 4, 8, 1, 3, 12]
PLACE = [ORDER.index(s) for s in range(GROUP)]
REACH_PLACE = [REACH.index(s) for s in range(GROUP)]
VMEM = pl.BlockSpec(memory_space=pltpu.VMEM)
SMEM = pl.BlockSpec(memory_space=pltpu.SMEM)
ANY = pl.BlockSpec(memory_space=pl.ANY)


def moved(code, places):
    shard = code % GROUP
    place = shard
    for s in range(GROUP):
        place = jnp.where(shard == s, places[s], place)
    return place + code - shard


def by_place(code):
    return moved(code, PLACE)


def to_reach(code):
    return moved(code, REACH_PLACE)


def unit_rows(raw):
    raw = raw.astype(jnp.float32)
    return raw * lax.rsqrt(jnp.sum(raw * raw, axis=1, keepdims=True) + 1e-06)


def normalise(partners_ref, counts_ref, doc_ref, unit, partners, counts, small_sem):
    small = [
        pltpu.make_async_copy(partners_ref, partners, small_sem.at[0]),
        pltpu.make_async_copy(counts_ref, counts, small_sem.at[1]),
    ]
    for copy in small:
        copy.start()
    for copy in small:
        copy.wait()
    lane = lax.broadcasted_iota(jnp.int32, (LIST, LANES), 1)
    entry = jnp.where(lane == 0, by_place(partners[0, 0]), 0)
    for p in range(1, PAIRS):
        entry = jnp.where(lane == p, by_place(partners[0, p]), entry)
    entry = entry.astype(jnp.float32).astype(jnp.bfloat16)
    for i in range(0, ROWS, STEP):
        rows = unit_rows(doc_ref[i : i + STEP])
        if i == 0:
            first = rows[:1]
        row = i + lax.broadcasted_iota(jnp.int32, (STEP, 1), 0)
        rows = jnp.where(row < counts[0], rows, first).astype(jnp.bfloat16)
        for j in range(0, STEP, CUT):
            at = (i + j) // CUT
            for t in range(TILES):
                unit[at, t * CUT : (t + 1) * CUT] = rows[j : j + CUT, t * LANES : (t + 1) * LANES]
            last = rows[j + CUT - (16 - LIST) : j + CUT, D - LANES :]
            unit[at, TALL - 16 :] = jnp.concatenate([last, entry])


def pick(table_ref, info_ref, own_ref, near_ref, far_ref, out_ref):
    def all_from(next_ref):
        for e in range(GROUP * SLOTS):
            dst, slot = e // SLOTS, e % SLOTS
            code = table_ref[dst * PAIRS + 1 + slot]

            @pl.when(code < GROUP)
            def _():
                out_ref[dst, slot] = own_ref[code, :BODY]

            @pl.when(code >= GROUP)
            def _():
                out_ref[dst, slot] = next_ref[code - GROUP, :BODY]

    @pl.when(info_ref[0] == 0)
    def _():
        all_from(near_ref)

    @pl.when(info_ref[0] == 1)
    def _():
        all_from(far_ref)


def rows_of(slices):
    tiles = [slices[:, t * CUT : (t + 1) * CUT].reshape(ROWS, LANES) for t in range(TILES)]
    return jnp.concatenate(tiles, axis=1)


def products(left, right):
    return lax.dot_general(left, right, (((1,), (1,)), ((), ())), preferred_element_type=jnp.float32)


def folded(part, rows):
    for t in range(rows.shape[1] // 128):
        part = jnp.maximum(part, rows[:, t * 128 : (t + 1) * 128])
    return part


def self_part(count, unit):
    row = lax.broadcasted_iota(jnp.int32, (ROWS, 1), 0)
    col = lax.broadcasted_iota(jnp.int32, (1, ROWS), 1)
    rows = jnp.where(jnp.logical_and(col < count, row != col), products(unit, unit), -1.0)
    return folded(jnp.full((ROWS, 128), -1.0, jnp.float32), rows)


def highest(part):
    return jnp.max(part.T, axis=0, keepdims=True)


def odd_self(info_ref, unit_ref, best_ref):
    @pl.when(info_ref[0] == 1)
    def _():
        best_ref[...] = highest(self_part(info_ref[2 + PAIRS], rows_of(unit_ref)))

    @pl.when(info_ref[0] == 0)
    def _():
        best_ref[...] = jnp.full(best_ref.shape, -1.0, jnp.float32)


def pair_scores(info_ref, unit_ref, got_ref, send_ref, over_ref=None):
    odd, mine = info_ref[0], info_ref[1]
    unit = rows_of(unit_ref)
    send_ref[...] = jnp.full(send_ref.shape, -1.0, jnp.float32)
    part = jnp.full((ROWS, 128), -1.0, jnp.float32)
    for p in range(SLOTS):
        code = info_ref[3 + p]
        twice = code == mine
        scores = products(unit, rows_of(got_ref.at[:, p]))
        part = jnp.where(twice, part, folded(part, scores))
        cols = jnp.where(twice, -1.0, jnp.max(scores, axis=0, keepdims=True))
        line = to_reach(code) + jnp.where(odd == 1, 0, GROUP)

        @pl.when(line < 2 * GROUP)
        def _():
            send_ref[line] = jnp.maximum(send_ref[line], cols)

        if over_ref is not None:

            @pl.when(line >= 2 * GROUP)
            def _():
                over_ref[line - 2 * GROUP] = jnp.maximum(over_ref[line - 2 * GROUP], cols)

    return part


def even_scores(info_ref, unit_ref, got_ref, best_ref, send_ref, over_ref):
    over_ref[...] = jnp.full(over_ref.shape, -1.0, jnp.float32)

    @pl.when(info_ref[0] == 0)
    def _():
        part = pair_scores(info_ref, unit_ref, got_ref, send_ref, over_ref)
        best_ref[...] = highest(jnp.maximum(part, self_part(info_ref[2 + PAIRS], rows_of(unit_ref))))


def odd_scores(info_ref, unit_ref, got_ref, self_ref, held_best_ref, held_send_ref, best_ref, send_ref):
    @pl.when(info_ref[0] == 1)
    def _():
        part = pair_scores(info_ref, unit_ref, got_ref, send_ref)
        best_ref[...] = jnp.maximum(highest(part), self_ref[...])

    @pl.when(info_ref[0] == 0)
    def _():
        best_ref[...] = held_best_ref[...]
        send_ref[...] = held_send_ref[...]


def exchange(parts):
    return lax.all_to_all(parts, "shard", 0, 0, axis_index_groups=[ORDER], tiled=True)


def shards(documents, partners, counts):
    n_cluster = lax.axis_size("cluster")
    my_cluster, my_shard = lax.axis_index("cluster"), lax.axis_index("shard")
    odd = my_cluster % 2
    unit = pl.pallas_call(
        normalise,
        in_specs=[ANY, ANY, VMEM],
        out_specs=VMEM,
        out_shape=jax.ShapeDtypeStruct((GROUP, TALL, LANES), jnp.bfloat16),
        scratch_shapes=[
            pltpu.SMEM((1, PAIRS), jnp.int32),
            pltpu.SMEM((1,), jnp.int32),
            pltpu.SemaphoreType.DMA((2,)),
        ],
        compiler_params=pltpu.CompilerParams(vmem_limit_bytes=8 * 2**20),
    )(partners, counts, documents)
    own = exchange(unit)
    near = lax.ppermute(own, "cluster", [(c, c ^ 1) for c in range(n_cluster)])
    info = jnp.concatenate([odd[None], my_shard[None], partners[0], counts])
    held, own = lax.optimization_barrier((unit, own))
    self_best = pl.pallas_call(
        odd_self,
        in_specs=[SMEM, VMEM],
        out_specs=VMEM,
        out_shape=jax.ShapeDtypeStruct((1, ROWS), jnp.float32),
        cost_estimate=pl.CostEstimate(flops=2 * ROWS * ROWS * D, bytes_accessed=ROWS * D * 2, transcendentals=0),
        compiler_params=pltpu.CompilerParams(vmem_limit_bytes=12 * 2**20),
    )(info, held)
    table = own[:, BODY, :PAIRS].astype(jnp.int32).reshape(-1)
    near, self_best, table, info, is_odd = lax.optimization_barrier((near, self_best, table, info, odd == 1))
    far = lax.ppermute(near, "cluster", [((c + 2) % n_cluster, c) for c in range(1, n_cluster, 2)])
    picked = pl.pallas_call(
        pick,
        in_specs=[SMEM, SMEM, VMEM, VMEM, VMEM],
        out_specs=VMEM,
        out_shape=jax.ShapeDtypeStruct((GROUP, SLOTS, BODY, LANES), jnp.bfloat16),
        compiler_params=pltpu.CompilerParams(vmem_limit_bytes=8 * 2**20),
    )(table, info, own, near, far)
    picked, info, self_best, is_odd = lax.optimization_barrier((picked, info, self_best, is_odd))
    got = exchange(picked)
    best_shape = jax.ShapeDtypeStruct((1, ROWS), jnp.float32)
    send_shape = jax.ShapeDtypeStruct((2 * GROUP, 1, ROWS), jnp.float32)
    over_shape = jax.ShapeDtypeStruct((GROUP, 1, ROWS), jnp.float32)
    params = pltpu.CompilerParams(vmem_limit_bytes=12 * 2**20)
    best, send, over = pl.pallas_call(
        even_scores,
        in_specs=[SMEM, VMEM, VMEM],
        out_specs=[VMEM] * 3,
        out_shape=[best_shape, send_shape, over_shape],
        compiler_params=params,
    )(info, unit, got)
    over = lax.ppermute(over, "cluster", [(c, c ^ 1) for c in range(n_cluster)])
    best, send = pl.pallas_call(
        odd_scores,
        in_specs=[SMEM] + [VMEM] * 5,
        out_specs=[VMEM] * 2,
        out_shape=[best_shape, send_shape],
        input_output_aliases={4: 0, 5: 1},
        compiler_params=params,
        cost_estimate=pl.CostEstimate(flops=SLOTS * 2 * ROWS * ROWS * D, bytes_accessed=4 * ROWS * D * 2, transcendentals=0),
    )(info, unit, got, self_best, best, send)
    first = jnp.where(is_odd, jnp.maximum(send[:GROUP], over), send[:GROUP])
    send = jnp.concatenate([first, send[GROUP:]])
    reach = [
        [c * GROUP + s for c in (odd_one, (odd_one + 1) % n_cluster) for s in REACH]
        for odd_one in range(1, n_cluster, 2)
    ]
    back = lax.all_to_all(send, ("cluster", "shard"), 0, 0, axis_index_groups=reach, tiled=True)
    best = jnp.maximum(best[0], jnp.max(back, axis=(0, 1)))
    return jnp.where(jnp.arange(ROWS, dtype=jnp.int32) < counts[0], best, 0.0)


def solution(mesh):
    return jax.shard_map(
        shards,
        mesh=mesh,
        in_specs=(
            P(("cluster", "shard"), None),
            P(("cluster", "shard"), None),
            P(("cluster", "shard")),
        ),
        out_specs=P(("cluster", "shard")),
        check_vma=False,
    )
```

```python
import jax
import jax.numpy as jnp
from jax import lax
from jax.experimental import pallas as pl
from jax.experimental.pallas import tpu as pltpu
from jax.sharding import PartitionSpec as P

ROWS = 512
D = 1024
PAIRS = 4
SLOTS = PAIRS - 1
GROUP = 16
CUT = ROWS // GROUP
LANES = 128
TILES = D // LANES
BODY = TILES * CUT
LIST = 8
TALL = BODY + LIST
STEP = 256
ORDER = [10, 15, 13, 11, 12, 14, 6, 7, 0, 9, 5, 4, 8, 1, 3, 2]
REACH = ORDER
PLACE = [ORDER.index(s) for s in range(GROUP)]
REACH_PLACE = [REACH.index(s) for s in range(GROUP)]
VMEM = pl.BlockSpec(memory_space=pltpu.VMEM)
SMEM = pl.BlockSpec(memory_space=pltpu.SMEM)
ANY = pl.BlockSpec(memory_space=pl.ANY)


def moved(code, places):
    shard = code % GROUP
    place = shard
    for s in range(GROUP):
        place = jnp.where(shard == s, places[s], place)
    return place + code - shard


def by_place(code):
    return moved(code, PLACE)


def to_reach(code):
    return moved(code, REACH_PLACE)


def unit_rows(raw):
    raw = raw.astype(jnp.float32)
    return raw * lax.rsqrt(jnp.sum(raw * raw, axis=1, keepdims=True) + 1e-06)


def normalise(partners_ref, counts_ref, doc_ref, unit, partners, counts, small_sem):
    small = [
        pltpu.make_async_copy(partners_ref, partners, small_sem.at[0]),
        pltpu.make_async_copy(counts_ref, counts, small_sem.at[1]),
    ]
    for copy in small:
        copy.start()
    for copy in small:
        copy.wait()
    lane = lax.broadcasted_iota(jnp.int32, (LIST, LANES), 1)
    entry = jnp.where(lane == 0, by_place(partners[0, 0]), 0)
    for p in range(1, PAIRS):
        entry = jnp.where(lane == p, by_place(partners[0, p]), entry)
    entry = entry.astype(jnp.float32).astype(jnp.bfloat16)
    for i in range(0, ROWS, STEP):
        rows = unit_rows(doc_ref[i : i + STEP])
        if i == 0:
            first = rows[:1]
        row = i + lax.broadcasted_iota(jnp.int32, (STEP, 1), 0)
        rows = jnp.where(row < counts[0], rows, first).astype(jnp.bfloat16)
        for j in range(0, STEP, CUT):
            at = (i + j) // CUT
            for t in range(TILES):
                unit[at, t * CUT : (t + 1) * CUT] = rows[j : j + CUT, t * LANES : (t + 1) * LANES]
            last = rows[j + CUT - (16 - LIST) : j + CUT, D - LANES :]
            unit[at, TALL - 16 :] = jnp.concatenate([last, entry])


def pick(table_ref, info_ref, own_ref, near_ref, far_ref, out_ref):
    def all_from(next_ref):
        for e in range(GROUP * SLOTS):
            dst, slot = e // SLOTS, e % SLOTS
            code = table_ref[dst * PAIRS + 1 + slot]

            @pl.when(code < GROUP)
            def _():
                out_ref[dst, slot] = own_ref[code, :BODY]

            @pl.when(code >= GROUP)
            def _():
                out_ref[dst, slot] = next_ref[code - GROUP, :BODY]

    @pl.when(info_ref[0] == 0)
    def _():
        all_from(near_ref)

    @pl.when(info_ref[0] == 1)
    def _():
        all_from(far_ref)


def rows_of(slices):
    tiles = [slices[:, t * CUT : (t + 1) * CUT].reshape(ROWS, LANES) for t in range(TILES)]
    return jnp.concatenate(tiles, axis=1)


def products(left, right):
    return lax.dot_general(left, right, (((1,), (1,)), ((), ())), preferred_element_type=jnp.float32)


def folded(part, rows):
    for t in range(rows.shape[1] // 128):
        part = jnp.maximum(part, rows[:, t * 128 : (t + 1) * 128])
    return part


def self_part(count, unit):
    row = lax.broadcasted_iota(jnp.int32, (ROWS, 1), 0)
    col = lax.broadcasted_iota(jnp.int32, (1, ROWS), 1)
    rows = jnp.where(jnp.logical_and(col < count, row != col), products(unit, unit), -1.0)
    return folded(jnp.full((ROWS, 128), -1.0, jnp.float32), rows)


def highest(part):
    return jnp.max(part.T, axis=0, keepdims=True)


def odd_self(info_ref, unit_ref, best_ref):
    @pl.when(info_ref[0] == 1)
    def _():
        best_ref[...] = highest(self_part(info_ref[2 + PAIRS], rows_of(unit_ref)))

    @pl.when(info_ref[0] == 0)
    def _():
        best_ref[...] = jnp.full(best_ref.shape, -1.0, jnp.float32)


def pair_scores(info_ref, unit_ref, got_ref, send_ref, over_ref=None):
    odd, mine = info_ref[0], info_ref[1]
    unit = rows_of(unit_ref)
    send_ref[...] = jnp.full(send_ref.shape, -1.0, jnp.float32)
    part = jnp.full((ROWS, 128), -1.0, jnp.float32)
    for p in range(SLOTS):
        code = info_ref[3 + p]
        twice = code == mine
        scores = products(unit, rows_of(got_ref.at[:, p]))
        part = jnp.where(twice, part, folded(part, scores))
        cols = jnp.where(twice, -1.0, jnp.max(scores, axis=0, keepdims=True))
        line = to_reach(code) + jnp.where(odd == 1, 0, GROUP)

        @pl.when(line < 2 * GROUP)
        def _():
            send_ref[line] = jnp.maximum(send_ref[line], cols)

        if over_ref is not None:

            @pl.when(line >= 2 * GROUP)
            def _():
                over_ref[line - 2 * GROUP] = jnp.maximum(over_ref[line - 2 * GROUP], cols)

    return part


def even_scores(info_ref, unit_ref, got_ref, best_ref, send_ref, over_ref):
    over_ref[...] = jnp.full(over_ref.shape, -1.0, jnp.float32)

    @pl.when(info_ref[0] == 0)
    def _():
        part = pair_scores(info_ref, unit_ref, got_ref, send_ref, over_ref)
        best_ref[...] = highest(jnp.maximum(part, self_part(info_ref[2 + PAIRS], rows_of(unit_ref))))


def odd_scores(info_ref, unit_ref, got_ref, self_ref, held_best_ref, held_send_ref, best_ref, send_ref):
    @pl.when(info_ref[0] == 1)
    def _():
        part = pair_scores(info_ref, unit_ref, got_ref, send_ref)
        best_ref[...] = jnp.maximum(highest(part), self_ref[...])

    @pl.when(info_ref[0] == 0)
    def _():
        best_ref[...] = held_best_ref[...]
        send_ref[...] = held_send_ref[...]


def exchange(parts):
    return lax.all_to_all(parts, "shard", 0, 0, axis_index_groups=[ORDER], tiled=True)


def shards(documents, partners, counts):
    n_cluster = lax.axis_size("cluster")
    my_cluster, my_shard = lax.axis_index("cluster"), lax.axis_index("shard")
    odd = my_cluster % 2
    unit = pl.pallas_call(
        normalise,
        in_specs=[ANY, ANY, VMEM],
        out_specs=VMEM,
        out_shape=jax.ShapeDtypeStruct((GROUP, TALL, LANES), jnp.bfloat16),
        scratch_shapes=[
            pltpu.SMEM((1, PAIRS), jnp.int32),
            pltpu.SMEM((1,), jnp.int32),
            pltpu.SemaphoreType.DMA((2,)),
        ],
        compiler_params=pltpu.CompilerParams(vmem_limit_bytes=8 * 2**20),
    )(partners, counts, documents)
    own = exchange(unit)
    near = lax.ppermute(own, "cluster", [(c, c ^ 1) for c in range(n_cluster)])
    info = jnp.concatenate([odd[None], my_shard[None], partners[0], counts])
    held, own = lax.optimization_barrier((unit, own))
    self_best = pl.pallas_call(
        odd_self,
        in_specs=[SMEM, VMEM],
        out_specs=VMEM,
        out_shape=jax.ShapeDtypeStruct((1, ROWS), jnp.float32),
        cost_estimate=pl.CostEstimate(flops=2 * ROWS * ROWS * D, bytes_accessed=ROWS * D * 2, transcendentals=0),
        compiler_params=pltpu.CompilerParams(vmem_limit_bytes=12 * 2**20),
    )(info, held)
    table = own[:, BODY, :PAIRS].astype(jnp.int32).reshape(-1)
    near, self_best, table, info, is_odd = lax.optimization_barrier((near, self_best, table, info, odd == 1))
    far = lax.ppermute(near, "cluster", [((c + 2) % n_cluster, c) for c in range(1, n_cluster, 2)])
    picked = pl.pallas_call(
        pick,
        in_specs=[SMEM, SMEM, VMEM, VMEM, VMEM],
        out_specs=VMEM,
        out_shape=jax.ShapeDtypeStruct((GROUP, SLOTS, BODY, LANES), jnp.bfloat16),
        compiler_params=pltpu.CompilerParams(vmem_limit_bytes=8 * 2**20),
    )(table, info, own, near, far)
    picked, info, self_best, is_odd = lax.optimization_barrier((picked, info, self_best, is_odd))
    got = exchange(picked)
    best_shape = jax.ShapeDtypeStruct((1, ROWS), jnp.float32)
    send_shape = jax.ShapeDtypeStruct((2 * GROUP, 1, ROWS), jnp.float32)
    over_shape = jax.ShapeDtypeStruct((GROUP, 1, ROWS), jnp.float32)
    params = pltpu.CompilerParams(vmem_limit_bytes=12 * 2**20)
    best, send, over = pl.pallas_call(
        even_scores,
        in_specs=[SMEM, VMEM, VMEM],
        out_specs=[VMEM] * 3,
        out_shape=[best_shape, send_shape, over_shape],
        compiler_params=params,
    )(info, unit, got)
    over = lax.ppermute(over, "cluster", [(c, c ^ 1) for c in range(n_cluster)])
    best, send = pl.pallas_call(
        odd_scores,
        in_specs=[SMEM] + [VMEM] * 5,
        out_specs=[VMEM] * 2,
        out_shape=[best_shape, send_shape],
        input_output_aliases={4: 0, 5: 1},
        compiler_params=params,
        cost_estimate=pl.CostEstimate(flops=SLOTS * 2 * ROWS * ROWS * D, bytes_accessed=4 * ROWS * D * 2, transcendentals=0),
    )(info, unit, got, self_best, best, send)
    first = jnp.where(is_odd, jnp.maximum(send[:GROUP], over), send[:GROUP])
    send = jnp.concatenate([first, send[GROUP:]])
    reach = [
        [c * GROUP + s for c in (odd_one, (odd_one + 1) % n_cluster) for s in REACH]
        for odd_one in range(1, n_cluster, 2)
    ]
    back = lax.all_to_all(send, ("cluster", "shard"), 0, 0, axis_index_groups=reach, tiled=True)
    best = jnp.maximum(best[0], jnp.max(back, axis=(0, 1)))
    return jnp.where(jnp.arange(ROWS, dtype=jnp.int32) < counts[0], best, 0.0)


def solution(mesh):
    return jax.shard_map(
        shards,
        mesh=mesh,
        in_specs=(
            P(("cluster", "shard"), None),
            P(("cluster", "shard"), None),
            P(("cluster", "shard")),
        ),
        out_specs=P(("cluster", "shard")),
        check_vma=False,
    )
```
